256 devices in a mesh: req: 16 (over z, core), seq: 16 (over y, x).
Axes of the slice: x: 4, y: 4, z: 8, core: 2. Of those that a mesh axis runs over, the one named last changes fastest.
Arguments:
- kv_pool: float32 [16, 768, 2, 16, 512], P('req', 'seq'), may hold values from -10 to 10
- page_owner: int32 [4, 16, 192], P(None, 'req'), may hold values from 0 to 15, as said below
- page_slot: int32 [4, 16, 192], P(None, 'req'), may hold values from 0 to 47
- lengths: int32 [4, 16], P(None, 'req'), may hold values from 16 to 3072, as said below
- queries: float32 [4, 16, 4, 16, 256], P(None, 'req'), may hold values from -100 to 100
- gates: bfloat16 [4, 16, 4, 16, 256], P(None, 'req'), may hold values from -6 to 6
- new_kv: float32 [4, 16, 4, 2, 2, 256], P(None, 'req'), may hold values from -8 to 8
- tokens: bfloat16 [4, 16, 4, 2048], P(None, 'req'), may hold values from -6 to 6
- attn_gain: float32 [2048], replicated, may hold values from 0.1 to 1.9
- out_heads: bfloat16 [16, 256, 2048], P('seq'), may hold values from -0.09375 to 0.09375
- w_query_key: bfloat16 [2048, 16, 2, 128], P(None, 'seq'), may hold values from -0.125 to 0.125
- w_value_gate: bfloat16 [2048, 32, 2, 128], P(None, 'seq'), may hold values from -0.125 to 0.125
- w_beta_decay: bfloat16 [2048, 2, 32], P(None, None, 'seq'), may hold values from -0.125 to 0.125
- decay_scale: float32 [32], P('seq'), may hold values from 0.02 to 2
- dt_bias: float32 [32], P('seq'), may hold values from -2 to 2
- delta_gain: float32 [128], replicated, may hold values from 0.1 to 1.9
- w_delta_out: bfloat16 [32, 128, 2048], P('seq'), may hold values from -0.09375 to 0.09375
- prior_state: float32 [4, 16, 32, 128, 128], P(None, None, 'req', 'seq'), may hold values from -1.5 to 1.5
Outputs:
- layer_output: float32 [4, 16, 4, 2048], P(None, 'req', None, 'seq')
The draws below stay inside these ranges and needn't reach their ends.
Inputs may be any that keep to these rules, and one draw needn't show every extreme that they name: In each request group g the pairs (page_owner, page_slot) over its 4 requests and 192 pages are all distinct, so each of the 16 owners holds exactly 48 of the group's pages and each share j // 12 of the sequence split covers exactly 48 pages. The pages of one group from one owner to one share number at most 6; every group has an owner and a share with exactly 6. `lengths`: both ends of the range occur in every draw.
All inputs are finite; a program needn't handle non-finite values.
Results may differ from the reference program's by a relative error of at most 0.005.
Values may be sent and summed in bfloat16 or wider, within the bound.
A program may use at most 128 MiB of HBM per device.

```python
import math
import jax
import jax.numpy as jnp
from jax import lax

D = 2048
QH = 16
KVH = 2
HD = 256
KH = 16
VH = 32
DK = 128
DV = 128
STEPS = 4
PAGE = 16
R_DEV = 4
PD = 12
NP = 192
N_REQ = 16
N_SEQ = 16


def page_tables(key):
    slot_count = R_DEV * PD
    even_share = slot_count // N_SEQ
    indices = jnp.arange(N_SEQ, dtype=jnp.int32)

    def placed(mapping):
        return (mapping[:, None] == indices[None, :]).astype(jnp.int32)

    def shuffle(part_key):
        return jax.random.permutation(part_key, slot_count).astype(jnp.int32)

    def one_group(group_key):
        subkeys = jax.random.split(group_key, 6)
        leading = jax.random.permutation(subkeys[0], N_SEQ).astype(jnp.int32)
        pinned = jnp.concatenate([jnp.zeros((1,), jnp.int32), 1 + jax.random.permutation(subkeys[1], N_SEQ - 1).astype(jnp.int32)])
        second = leading[pinned]
        amount = jax.random.randint(subkeys[2], (), 0, even_share + 1)
        matrix = even_share + amount * (placed(leading) - placed(jnp.roll(leading, -1))) + (even_share - amount) * (placed(second) - placed(jnp.roll(second, -1)))
        matrix = matrix[jax.random.permutation(subkeys[3], N_SEQ)]
        bounds = jnp.cumsum(matrix, axis=0)
        position = jnp.arange(slot_count, dtype=jnp.int32)
        owners = jnp.sum((bounds[None, :, :] <= position[:, None, None]).astype(jnp.int32), axis=1)
        shuffles = jax.vmap(shuffle)(jax.random.split(subkeys[4], N_SEQ))
        shuffled = jnp.take_along_axis(owners, shuffles.T, axis=0)
        owner_table = shuffled.reshape(R_DEV, PD, N_SEQ).transpose(0, 2, 1).reshape(R_DEV, PD * N_SEQ)
        flattened = owner_table.reshape(-1)
        matches = placed(flattened)
        ranking = jnp.sum((jnp.cumsum(matches, axis=0) - matches) * matches, axis=1)
        slot_perms = jax.vmap(shuffle)(jax.random.split(subkeys[5], N_SEQ))
        slot_table = slot_perms[flattened, ranking].reshape(R_DEV, PD * N_SEQ)
        return (owner_table, slot_table)

    def keyed_group(group):
        return one_group(jax.random.fold_in(key, group))
    owner_all, slot_all = jax.vmap(keyed_group)(jnp.arange(N_REQ))
    return (jnp.transpose(owner_all, (1, 0, 2)).astype(jnp.int32), jnp.transpose(slot_all, (1, 0, 2)).astype(jnp.int32))


def attention_inputs(key):
    query_shape = (R_DEV, N_REQ, STEPS, QH, HD)
    draft_shape = (R_DEV, N_REQ, STEPS, 2, KVH, HD)
    base_queries = jnp.clip(jax.random.normal(jax.random.fold_in(key, 101), query_shape, jnp.float32), -6.0, 6.0)
    drafts = jnp.clip(jax.random.normal(jax.random.fold_in(key, 102), draft_shape, jnp.float32), -6.0, 6.0)
    latest = base_queries[:, :, STEPS - 1]
    queries = base_queries.at[:, :, STEPS - 1].set(latest)
    early = queries[:, :, 1]
    queries = queries.at[:, :, 1].set(early)
    follow = drafts[:, :, 2, 0]
    drafts = drafts.at[:, :, 2, 0].set(follow)
    return (queries, drafts)


def draw_kv_pool(key, part):
    key = jax.random.fold_in(key, 5)
    shape = (N_REQ, N_SEQ * R_DEV * PD, 2, PAGE, KVH * HD)
    pool = jnp.clip(jax.random.normal(key, shape, jnp.float32), -6.0, 6.0)
    return pool


def draw_page_owner(key, part):
    return page_tables(key)[0]


def draw_page_slot(key, part):
    return page_tables(key)[1]


def draw_lengths(key, part):
    key = jax.random.fold_in(key, 7)
    subkeys = jax.random.split(key, 3)
    count_all = R_DEV * N_REQ
    longest = PD * N_SEQ * PAGE
    values = jax.random.randint(subkeys[0], (count_all,), PAGE, longest + 1)
    top_pick = jax.random.randint(subkeys[1], (), 0, count_all)
    low_pick = (top_pick + 1 + jax.random.randint(subkeys[2], (), 0, count_all - 1)) % count_all
    indices = jnp.arange(count_all)
    values = jnp.where(indices == top_pick, longest, values)
    values = jnp.where(indices == low_pick, PAGE, values)
    return values.reshape(R_DEV, N_REQ).astype(jnp.int32)


def draw_queries(key, part):
    return attention_inputs(key)[0]


def draw_new_kv(key, part):
    return attention_inputs(key)[1]


def shard_levels(stream_key, dims, pieces, least, largest):
    def one(axis_at, shards_of):
        heights = jax.random.uniform(jax.random.fold_in(jax.random.fold_in(stream_key, 6), axis_at), (shards_of,), jnp.float32, least / len(pieces), largest / len(pieces))
        return jnp.repeat(jnp.exp(heights), dims[axis_at] // shards_of).reshape((-1,) + (1,) * (len(dims) - axis_at - 1))

    loudness = one(*pieces[0])
    for cut in pieces[1:]:
        loudness = loudness * one(*cut)
    return loudness


def bell_draw(stream_key, dims, width, most, pieces=(), held_as=jnp.bfloat16):
    level = shard_levels(stream_key, dims, pieces, -0.22, 0.18) if pieces else 1.0
    values = jax.random.normal(stream_key, dims, jnp.float32) * width * level
    return jnp.minimum(jnp.maximum(values, -most), most).astype(held_as)


def setup_inputs(seed: int = 0) -> dict:
    key_list = jax.random.split(jax.random.key(seed), 19)
    kv_pool = draw_kv_pool(jax.random.fold_in(key_list[18], 71), 0)
    page_owner = draw_page_owner(jax.random.fold_in(key_list[18], 71), 0)
    page_slot = draw_page_slot(jax.random.fold_in(key_list[18], 71), 0)
    lengths = draw_lengths(jax.random.fold_in(key_list[18], 71), 0)
    queries = draw_queries(jax.random.fold_in(key_list[18], 71), 0)
    gates = bell_draw(key_list[5], (R_DEV, N_REQ, STEPS, QH, HD), 1.0, 6.0, ((1, 16),))
    new_kv = draw_new_kv(jax.random.fold_in(key_list[18], 71), 0)
    tokens = bell_draw(key_list[7], (R_DEV, N_REQ, STEPS, D), 1.0, 6.0, ((1, 16),))
    attn_gain = jnp.clip(1.0 + 0.18 * jax.random.normal(key_list[8], (D,), jnp.float32), 0.1, 1.9)
    out_heads = bell_draw(key_list[9], (QH, HD, D), (QH * HD) ** -0.5, 0.09375, ((0, 16),))
    w_query_key = bell_draw(key_list[10], (D, KH, 2, DK), D ** -0.5, 0.125, ((1, 16),))
    w_value_gate = bell_draw(key_list[11], (D, VH, 2, DV), D ** -0.5, 0.125, ((1, 16),))
    w_beta_decay = bell_draw(key_list[12], (D, 2, VH), D ** -0.5, 0.125, ((2, 16),))
    decay_scale = jnp.clip(jnp.exp(math.log(2.0) - 4.6051702 * jax.random.uniform(key_list[13], (VH,), jnp.float32) ** shard_levels(key_list[13], (VH,), ((0, 16),), -0.2, 0.2)), 0.02, 2.0)
    dt_bias = jnp.clip(jax.random.uniform(key_list[14], (VH,), jnp.float32, -2.0, 2.0) * shard_levels(key_list[14], (VH,), ((0, 16),), -0.4, 0.0), -2.0, 2.0)
    delta_gain = jnp.clip(1.0 + 0.18 * jax.random.normal(key_list[15], (DV,), jnp.float32), 0.1, 1.9)
    w_delta_out = bell_draw(key_list[16], (VH, DV, D), (VH * DV) ** -0.5, 0.09375, ((0, 16),))
    prior_state = bell_draw(key_list[17], (R_DEV, N_REQ, VH, DV, DK), 0.1, 1.5, ((2, 16), (3, 16)), jnp.float32)
    return {"kv_pool": kv_pool, "page_owner": page_owner, "page_slot": page_slot, "lengths": lengths, "queries": queries, "gates": gates, "new_kv": new_kv, "tokens": tokens, "attn_gain": attn_gain, "out_heads": out_heads, "w_query_key": w_query_key, "w_value_gate": w_value_gate, "w_beta_decay": w_beta_decay, "decay_scale": decay_scale, "dt_bias": dt_bias, "delta_gain": delta_gain, "w_delta_out": w_delta_out, "prior_state": prior_state}


floor_score = -1e+30
norm_eps = 1e-06
highest = lax.Precision.HIGHEST

def rms_scale(values):
    return values * lax.rsqrt(lax.optimization_barrier(jnp.mean(values * values, axis=-1, keepdims=True)) + norm_eps)

def unit_rows(values):
    return values * lax.rsqrt(lax.optimization_barrier(jnp.sum(values * values, axis=-1, keepdims=True)) + norm_eps)

def attend_group(pool_group, owner_group, slot_group, length_group, query_group, gate_group, draft_group):
    pool_rows = owner_group * (R_DEV * PD) + slot_group
    page_rows = pool_group[pool_rows]
    cache_keys = page_rows[:, :, 0].reshape(R_DEV, NP * PAGE, KVH, HD)
    cache_values = page_rows[:, :, 1].reshape(R_DEV, NP * PAGE, KVH, HD)
    grouped = QH // KVH
    grouped_queries = query_group.reshape(R_DEV, STEPS, KVH, grouped, HD)
    score_scale = HD ** (-0.5)
    cache_scores = jnp.einsum('rskgd,rtkd->rskgt', grouped_queries, cache_keys, precision=highest) * score_scale
    in_context = (jnp.arange(NP * PAGE, dtype=jnp.int32)[None, :] < length_group[:, None])[:, None, None, None, :]
    draft_scores = jnp.einsum('rskgd,rukd->rskgu', grouped_queries, draft_group[:, :, 0], precision=highest) * score_scale
    causal = (jnp.arange(STEPS)[:, None] >= jnp.arange(STEPS)[None, :])[None, :, None, None, :]
    row_max = jnp.maximum(lax.optimization_barrier(jnp.max(jnp.where(in_context, cache_scores, floor_score), axis=-1)), lax.optimization_barrier(jnp.max(jnp.where(causal, draft_scores, floor_score), axis=-1)))
    cache_weights = jnp.where(in_context, jnp.exp(cache_scores - row_max[..., None]), 0.0)
    draft_weights = jnp.where(causal, jnp.exp(draft_scores - row_max[..., None]), 0.0)
    denominator = lax.optimization_barrier(jnp.sum(cache_weights, axis=-1)) + lax.optimization_barrier(jnp.sum(draft_weights, axis=-1))
    weighted = jnp.einsum('rskgt,rtkd->rskgd', cache_weights, cache_values, precision=highest)
    weighted = weighted + jnp.einsum('rskgu,rukd->rskgd', draft_weights, draft_group[:, :, 1], precision=highest)
    attended = (weighted / denominator[..., None]).reshape(R_DEV, STEPS, QH, HD)
    return (attended * jax.nn.sigmoid(gate_group.astype(jnp.float32))).astype(jnp.bfloat16)

def reference(kv_pool, page_owner, page_slot, lengths, queries, gates, new_kv, tokens, attn_gain, out_heads, w_query_key, w_value_gate, w_beta_decay, decay_scale, dt_bias, delta_gain, w_delta_out, prior_state):
    row_count = R_DEV * STEPS

    def one_group(group_id):

        def select(array, axis):
            return lax.dynamic_index_in_dim(array, group_id, axis, keepdims=False)
        gated_heads = attend_group(select(kv_pool, 0), select(page_owner, 1), select(page_slot, 1), select(lengths, 1), select(queries, 1), select(gates, 1), select(new_kv, 1))
        attn_total = jnp.dot(gated_heads.reshape(row_count, QH * HD), out_heads.reshape(QH * HD, D), preferred_element_type=jnp.float32)
        stream = select(tokens, 1).reshape(row_count, D).astype(jnp.float32) + attn_total
        normed = (rms_scale(stream) * attn_gain).astype(jnp.bfloat16)
        head_ratio = VH // KH
        paired = jnp.dot(normed, w_query_key.reshape(D, KH * 2 * DK), preferred_element_type=jnp.float32).reshape(R_DEV, STEPS, KH, 2, DK)
        delta_query = jnp.repeat(unit_rows(paired[..., 0, :]), head_ratio, axis=2)
        delta_key = jnp.repeat(unit_rows(paired[..., 1, :]), head_ratio, axis=2)
        value_proj = jnp.dot(normed, w_value_gate.reshape(D, VH * 2 * DV), preferred_element_type=jnp.float32).reshape(R_DEV, STEPS, VH, 2, DV)
        mixing = jnp.dot(normed, w_beta_decay.reshape(D, 2 * VH), preferred_element_type=jnp.float32).reshape(R_DEV, STEPS, 2, VH)
        beta_gate = jax.nn.sigmoid(mixing[:, :, 0])
        decay_rate = jnp.exp(-decay_scale * jax.nn.softplus(mixing[:, :, 1] + dt_bias))
        state_now = select(prior_state, 1).astype(jnp.float32)
        outputs = []
        for step_id in range(STEPS):
            state_now = decay_rate[:, step_id, :, None, None] * state_now
            predicted = jnp.einsum('rhvk,rhk->rhv', state_now, delta_key[:, step_id], precision=highest)
            update = beta_gate[:, step_id, :, None] * (value_proj[:, step_id, :, 0] - predicted)
            state_now = state_now + update[..., :, None] * delta_key[:, step_id][..., None, :]
            outputs.append(jnp.einsum('rhvk,rhk->rhv', state_now, delta_query[:, step_id], precision=highest) * DK ** (-0.5))
        readout = jnp.stack(outputs, axis=1)
        normalized = (rms_scale(readout) * delta_gain * jax.nn.silu(value_proj[..., 1, :])).astype(jnp.bfloat16)
        delta_total = jnp.dot(normalized.reshape(row_count, VH * DV), w_delta_out.reshape(VH * DV, D), preferred_element_type=jnp.float32)
        return (stream + delta_total).reshape(R_DEV, STEPS, D)
    results = lax.map(one_group, jnp.arange(N_REQ, dtype=jnp.int32))
    return jnp.moveaxis(results, 0, 1)
```

```python
import jax
import jax.numpy as jnp
from jax import lax
from jax.experimental import pallas as pl
from jax.experimental.pallas import tpu as pltpu
from jax.sharding import PartitionSpec as P

floor_score = -1e30
norm_eps = 1e-06
MESH = pl.DeviceIdType.MESH
f32 = jnp.float32
bf16 = jnp.bfloat16

GROUP = 16
REQS = 4
STEPS = 4
ROWS = REQS * STEPS
SLOTS = 48
PAGE = 16
TOKENS = SLOTS * PAGE
PAGES = 192
HD = 256
D = 2048
SHARE = 128
KVH = 2
PER_KV = 8
MSG = HD + 128
OFFSETS = [(y, x) for y in range(4) for x in range(4) if y or x]
FAR_FIRST = sorted(OFFSETS, key=lambda o: -(min(o[0], 4 - o[0]) + min(o[1], 4 - o[1])))
PLACES = (1, 0, 3, 2, 6, 5, 7, 4)
ALONG_X = [(0, 2), (0, 1), (0, 3)]
ALONG_Y = [(2, 0), (1, 0), (3, 0)]


def dot(a, b):
    return jnp.dot(a, b, preferred_element_type=f32)


def dot_t(a, b):
    return lax.dot_general(a, b, (((1,), (1,)), ((), ())), preferred_element_type=f32)


def iota(shape, axis):
    return lax.broadcasted_iota(jnp.int32, shape, axis)


def shifted(x, by):
    return jnp.concatenate([x[-by:], x[:-by]], axis=0) if by else x


def kernel(
    kv_hbm, owner_hbm, slot_hbm, lengths, q_hbm, gates_hbm, new_hbm, tokens_hbm, gain_hbm, wo_hbm,
    wqk_hbm, wvg_hbm, wmix_hbm, decay_scale, dt_bias, dgain_hbm, wdo_hbm, state_hbm,
    out_ref,
    kv, owner, slot, q, gates, new, tokens, gain, wo, wqk, wvg, wmix, dgain, wdo, state,
    fq, fv, w_all, w_mix, s_out, s_in, m_out, m_in, a_out, a_in, x_out, x_in, stream,
    d_out, d_in, load_sem, send_sem, recv_sem, ready_sem,
):
    i = lax.axis_index("req")
    me = lax.axis_index("seq")

    loads = {}

    def load(name, src, dst):
        copy = pltpu.make_async_copy(src, dst, load_sem.at[len(loads)])
        copy.start()
        loads[name] = copy

    def rank(plane):
        level = 0
        for z, place in enumerate(PLACES):
            level = jnp.where(plane // 2 == z, place, level)
        return 2 * level + 1 - lax.rem(plane, 2)

    def peer(offset):
        y, x = offset
        return lax.rem(me // 4 + y, 4) * 4 + lax.rem(lax.rem(me, 4) + x, 4)

    my_rank = rank(i)
    barrier = pltpu.get_barrier_semaphore()

    def greet(where):
        pl.semaphore_signal(barrier, inc=1, device_id=where, device_id_type=MESH)

    def each_state_peer(use):
        for d in range(GROUP):
            use(d, lax.rem(i + d, GROUP))

    def each_state_source(use):
        for d in range(GROUP):
            source = lax.rem(me + d, GROUP)
            if d:
                use(source)
            else:

                @pl.when(i != me)
                def _():
                    use(source)

    for offset in FAR_FIRST:
        greet((i, peer(offset)))
    early_receiver = my_rank <= rank(me)

    @pl.when(early_receiver)
    def _():
        each_state_source(lambda source: greet((me, source)))

    def greet_later(d, g):
        @pl.when(rank(g) > my_rank)
        def _():
            greet((g, i))

    each_state_peer(greet_later)

    load("owner", owner_hbm, owner)
    load("slot", slot_hbm, slot)
    load("q", q_hbm.at[:, 0:128], q.at[0])
    load("q_more", q_hbm.at[:, 128:256], q.at[1])
    load("kv", kv_hbm, kv)
    load("state", state_hbm, state)
    load("gates", gates_hbm, gates)
    load("new", new_hbm, new)
    load("wo", wo_hbm, wo)
    load("tokens", tokens_hbm.at[:, 0], tokens)
    load("gain", gain_hbm, gain)
    load("wqk", wqk_hbm, wqk)
    load("wvg", wvg_hbm, wvg)
    load("wmix", wmix_hbm, wmix)
    load("dgain", dgain_hbm, dgain)
    load("wdo", wdo_hbm, wdo)

    loads["owner"].wait()
    loads["slot"].wait()
    page_at = iota((SLOTS, PAGES), 1)
    slot_at = iota((SLOTS, PAGES), 0)
    row_request = lax.rem(iota((SLOTS, 128), 1) // STEPS, REQS)
    counts = jnp.zeros((SLOTS, 128), f32)
    for r in range(REQS):
        live = jnp.clip(lengths[r] - page_at * PAGE, 0, PAGE)
        held = (owner[r] == me) & (slot[r] == slot_at)
        count = jnp.sum(jnp.where(held, live, 0).astype(f32), axis=1, keepdims=True)
        counts = jnp.where(row_request == r, count, counts)
    spread = (iota((SLOTS, TOKENS), 1) // PAGE == iota((SLOTS, TOKENS), 0)).astype(f32).astype(bf16)
    limit = lax.dot_general(
        counts.astype(bf16), spread, (((0,), (0,)), ((), ())), preferred_element_type=f32
    )
    in_page = lax.rem(iota((128, TOKENS), 1), PAGE).astype(f32)
    live_mask = in_page < limit

    def head_queries(h):
        halves = [q[half, pl.ds(h, ROWS, stride=GROUP), :] for half in range(2)]
        return jnp.concatenate(halves, axis=1) * (HD ** -0.5)

    loads["q"].wait()
    loads["q_more"].wait()
    loads["kv"].wait()
    stat_lane = iota((128, 128), 1)
    for k in range(KVH):
        queries = jnp.concatenate([head_queries(k * PER_KV + h) for h in range(PER_KV)], axis=0)
        q_hi = queries.astype(bf16)
        q_lo = (queries - q_hi.astype(f32)).astype(bf16)
        keys = kv[:, 0, :, k * HD : (k + 1) * HD].reshape(TOKENS, HD)
        k_hi = keys.astype(bf16)
        k_lo = (keys - k_hi.astype(f32)).astype(bf16)
        scores = dot_t(q_hi, k_hi) + (dot_t(q_lo, k_hi) + dot_t(q_hi, k_lo))
        scores = jnp.where(live_mask, scores, floor_score)
        top = jnp.max(scores, axis=1, keepdims=True).astype(bf16).astype(f32)
        weights = jnp.where(live_mask, jnp.exp(scores - top), 0.0).astype(bf16)
        total = jnp.sum(weights.astype(f32), axis=1, keepdims=True)
        values = kv[:, 1, :, k * HD : (k + 1) * HD].reshape(TOKENS, HD).astype(bf16)
        acc = dot(weights, values)
        total_hi = total.astype(bf16).astype(f32)
        stats = jnp.where(stat_lane == 0, top, jnp.where(stat_lane == 1, total_hi, total - total_hi))
        own = pl.ds(k * PER_KV, PER_KV)
        m_out[own, :, 0:HD] = acc.astype(bf16).reshape(PER_KV, ROWS, HD)
        m_out[own, :, HD:MSG] = stats.astype(bf16).reshape(PER_KV, ROWS, 128)

    own_state = (i == me).astype(jnp.int32)
    late_receiver = (my_rank > rank(me)).astype(jnp.int32)
    pl.semaphore_wait(barrier, GROUP + my_rank - own_state + GROUP * late_receiver)

    def send(src, dst, phase, where, sent_at=None):
        pltpu.make_async_remote_copy(
            src_ref=src,
            dst_ref=dst,
            send_sem=send_sem.at[phase if sent_at is None else sent_at],
            recv_sem=recv_sem.at[phase],
            device_id=where,
            device_id_type=MESH,
        ).start()

    def scatter(src, dst, phase):
        for n, offset in enumerate(FAR_FIRST):
            other = peer(offset)
            send(src.at[other], dst.at[n], phase, (i, other))

    def arrived(ref, phase):
        pltpu.make_async_copy(ref, ref, recv_sem.at[phase]).wait()

    def sent(ref, phase):
        pltpu.make_async_copy(ref, ref, send_sem.at[phase]).wait()

    scatter(m_out, m_in, 0)

    loads["state"].wait()
    for g in range(GROUP):
        s_out[g] = state[:, g].reshape(REQS * 2 * 8, 128).astype(bf16)

    def send_states(later):
        def one(g):
            @pl.when(rank(g) > my_rank if later else rank(g) < my_rank)
            def _():
                send(s_out.at[g], s_in.at[me], 1, (g, i))

        for d in range(GROUP):
            one(lax.rem(i + me + GROUP - d, GROUP))

    @pl.when(jnp.logical_not(early_receiver))
    def _():
        each_state_source(
            lambda source: pl.semaphore_signal(
                ready_sem, inc=1, device_id=(me, source), device_id_type=MESH
            )
        )

    send_states(False)

    @pl.when(i != me)
    def _():
        send(s_out.at[i], s_in.at[me], 1, (i, i), 5)

    @pl.when(i == me)
    def _():
        pltpu.make_async_copy(s_out.at[i], s_in.at[me], recv_sem.at[1]).start()

    loads["wqk"].wait()
    loads["wvg"].wait()
    chunk = 256

    def arrange(c, carry):
        rows = pl.ds(pl.multiple_of(c * chunk, chunk), chunk)
        fq[...] = wqk[pl.ds(pl.multiple_of(c * (2 * chunk), 2 * chunk), 2 * chunk), :].astype(f32)
        fv[...] = wvg[pl.ds(pl.multiple_of(c * (4 * chunk), 4 * chunk), 4 * chunk), :].astype(f32)
        for n in range(2):
            w_all[rows, n * 128 : (n + 1) * 128] = fq[pl.ds(n, chunk, stride=2), :].astype(bf16)
        for n in range(4):
            w_all[rows, (n + 2) * 128 : (n + 3) * 128] = fv[pl.ds(n, chunk, stride=4), :].astype(bf16)
        return carry

    lax.fori_loop(0, D // chunk, arrange, 0)
    loads["wmix"].wait()
    for n in range(2):
        w_mix[2 * n : 2 * n + 2, :] = wmix[n].astype(f32)

    loads["new"].wait()
    loads["gates"].wait()
    own_q = head_queries(me)
    low_kv = me < PER_KV

    def draft(component):
        both = new[:, component].astype(f32)
        return jnp.where(low_kv, both[:, 0], both[:, 1])

    draft_scores = lax.dot_general(
        own_q, draft(0), (((1,), (1,)), ((), ())),
        preferred_element_type=f32, precision=lax.Precision.HIGHEST,
    )
    row, col = iota((ROWS, ROWS), 0), iota((ROWS, ROWS), 1)
    causal = (row // STEPS == col // STEPS) & (col <= row)
    draft_scores = jnp.where(causal, draft_scores, floor_score)
    draft_top = jnp.max(draft_scores, axis=1, keepdims=True)
    draft_weights = jnp.where(causal, jnp.exp(draft_scores - draft_top), 0.0)
    draft_total = jnp.sum(draft_weights, axis=1, keepdims=True)
    draft_acc = lax.dot_general(
        draft_weights, draft(1), (((1,), (0,)), ((), ())),
        preferred_element_type=f32, precision=lax.Precision.HIGHEST,
    )
    own_gate = jnp.sum(
        jnp.where(iota((ROWS, GROUP, HD), 1) == me, gates[...].astype(f32), 0.0), axis=1
    )
    gate = jax.nn.sigmoid(own_gate)

    arrived(m_in, 0)
    parts = [m_out[me]] + [m_in[d] for d in range(GROUP - 1)]
    ceiling = draft_top
    for part in parts:
        ceiling = jnp.maximum(ceiling, part[:, HD : HD + 1].astype(f32))
    factor = jnp.exp(draft_top - ceiling)
    total = draft_total * factor
    acc = draft_acc * factor
    for part in parts:
        stats = part[:, HD:MSG].astype(f32)
        factor = jnp.exp(stats[:, 0:1] - ceiling)
        total = total + factor * (stats[:, 1:2] + stats[:, 2:3])
        acc = acc + factor * part[:, 0:HD].astype(f32)
    gated = (acc / total * gate).astype(bf16)

    loads["wo"].wait()
    halves = [slice(0, D // 2), slice(D // 2, D)]

    def send_half(src, dst, n, along, phase):
        for m, offset in enumerate(along):
            send(src.at[n], dst.at[n, m], phase, (i, peer(offset)))

    ways = (ALONG_X, ALONG_Y)
    sums = []
    for n in range(2):
        sums.append(dot(gated, wo[:, halves[n]]))
        a_out[n] = sums[n].astype(bf16)
        send_half(a_out, a_in, n, ways[n], 2 + n)
    @pl.when(my_rank < GROUP - 1)
    def _():
        pl.semaphore_wait(ready_sem, GROUP - 1 - my_rank)

    send_states(True)
    for n in range(2):
        arrived(a_in.at[n], 2 + n)
        sums[n] = sums[n] + (a_in[n, 0].astype(f32) + a_in[n, 1].astype(f32) + a_in[n, 2].astype(f32))
        x_out[n] = sums[n].astype(bf16)
        send_half(x_out, x_in, n, ways[1 - n], 6 + n)

    loads["tokens"].wait()
    own_tokens = tokens[...].astype(f32).reshape(ROWS, D)

    loads["gain"].wait()
    loads["dgain"].wait()
    loads["wdo"].wait()
    arrived(s_in, 1)

    handed = s_in[...].astype(f32).reshape(GROUP, REQS, 2, 8, 128)
    states = []
    for r in range(REQS):
        blocks = [handed[j, r, h] for h in range(2) for j in range(GROUP)]
        states.append(jnp.concatenate(blocks, axis=0).astype(bf16))

    squares = jnp.zeros((ROWS, 1), f32)
    proj = jnp.zeros((ROWS, 6 * 128), f32)
    mixes = [jnp.zeros((ROWS, 1), f32) for _ in range(4)]
    for n in range(2):
        arrived(x_in.at[n], 6 + n)
        x = own_tokens[:, halves[n]] + (
            sums[n] + (x_in[n, 0].astype(f32) + x_in[n, 1].astype(f32) + x_in[n, 2].astype(f32))
        )
        stream[:, halves[n]] = x
        squares = squares + jnp.sum(x * x, axis=1, keepdims=True)
        y = (x * gain[:, halves[n]]).astype(bf16)
        proj = proj + dot(y, w_all[halves[n], :])
        y = y.astype(f32)
        for c in range(4):
            mixes[c] = mixes[c] + jnp.sum(y * w_mix[c : c + 1, halves[n]], axis=1, keepdims=True)
    scale = lax.rsqrt(squares * (1.0 / D) + norm_eps)
    proj = proj * scale
    mixes = [mix * scale for mix in mixes]

    def unit(x):
        return x * lax.rsqrt(jnp.sum(x * x, axis=1, keepdims=True) + norm_eps)

    dq = unit(proj[:, 0:128])
    dk = unit(proj[:, 128:256])
    value = jnp.concatenate([proj[:, 256:384], proj[:, 512:640]], axis=1)
    zgate = jnp.concatenate([proj[:, 384:512], proj[:, 640:768]], axis=1)
    high = iota((ROWS, 2 * 128), 1) >= 128
    beta = jnp.where(high, jax.nn.sigmoid(mixes[1]), jax.nn.sigmoid(mixes[0]))

    def decay_of(h):
        t = mixes[2 + h] + dt_bias[h]
        soft = jnp.maximum(t, 0.0) + jnp.log(1.0 + jnp.exp(-jnp.abs(t)))
        return jnp.exp(-decay_scale[h] * soft)

    decay = jnp.where(high, decay_of(1), decay_of(0))

    both = jnp.concatenate([dk, dq], axis=0).astype(bf16)
    row_of = lax.rem(iota((2 * ROWS, 2 * 128), 0) // STEPS, REQS)
    prior = jnp.zeros((2 * ROWS, 2 * 128), f32)
    for r in range(REQS):
        prior = jnp.where(row_of == r, dot_t(both, states[r]), prior)
    prior_k, prior_q = prior[:ROWS], prior[ROWS:]
    step = lax.rem(iota((ROWS, 2 * 128), 0), STEPS)
    ratio = [jnp.ones((ROWS, 2 * 128), f32), decay]
    for o in range(1, STEPS):
        ratio.append(decay * shifted(ratio[o], 1))
    whole = jnp.where(step == 0, ratio[1], jnp.where(step == 1, ratio[2], jnp.where(step == 2, ratio[3], ratio[4])))
    key_back = [shifted(dk, o) for o in range(STEPS)]
    beta_prior = beta * (value - whole * prior_k)
    coupling = [
        jnp.where(step >= o, beta * ratio[o] * jnp.sum(dk * key_back[o], axis=1, keepdims=True), 0.0)
        for o in range(1, STEPS)
    ]
    update = beta_prior
    for _ in range(STEPS - 1):
        following = beta_prior
        for o in range(1, STEPS):
            following = following - coupling[o - 1] * shifted(update, o)
        update = following
    readout = whole * prior_q
    for o in range(STEPS):
        reach = jnp.sum(dq * key_back[o], axis=1, keepdims=True)
        readout = readout + jnp.where(step >= o, ratio[o] * reach, 0.0) * shifted(update, o)
    readout = readout * (128 ** -0.5)

    def normal(x):
        return x * lax.rsqrt(jnp.mean(x * x, axis=1, keepdims=True) + norm_eps) * dgain[...]

    normalized = jnp.concatenate([normal(readout[:, :128]), normal(readout[:, 128:])], axis=1)
    normalized = (normalized * zgate * jax.nn.sigmoid(zgate)).astype(bf16)

    total = dot(normalized, wdo[...])
    for e in range(GROUP):
        d_out[e] = total[:, e * SHARE : (e + 1) * SHARE].astype(bf16)
    scatter(d_out, d_in, 4)
    own_lanes = pl.ds(pl.multiple_of(me * SHARE, SHARE), SHARE)
    result = stream[:, own_lanes] + d_out[me].astype(f32)
    sent(m_in, 0)
    sent(s_in.at[pl.ds(0, GROUP - 1)], 1)

    @pl.when(i != me)
    def _():
        sent(s_in.at[0], 5)

    for n in range(2):
        sent(a_in.at[n], 2 + n)
        sent(x_in.at[n], 6 + n)
    arrived(d_in, 4)
    for d in range(GROUP - 1):
        result = result + d_in[d].astype(f32)
    out_ref[...] = result
    sent(d_in, 4)


def body(
    kv_pool, page_owner, page_slot, lengths, queries, gates, new_kv, tokens, attn_gain, out_heads,
    w_query_key, w_value_gate, w_beta_decay, decay_scale, dt_bias, delta_gain, w_delta_out, prior_state,
):
    hbm = pl.BlockSpec(memory_space=pl.ANY)
    smem = pl.BlockSpec(memory_space=pltpu.SMEM)
    vmem = pltpu.VMEM
    operands = (
        (kv_pool.reshape(SLOTS, 2, PAGE, KVH * HD), hbm),
        (page_owner, hbm),
        (page_slot, hbm),
        (lengths.reshape(REQS), smem),
        (queries.reshape(ROWS * GROUP, HD), hbm),
        (gates.reshape(ROWS, GROUP, HD), hbm),
        (new_kv.reshape(ROWS, 2, KVH, HD), hbm),
        (tokens, hbm),
        (attn_gain.reshape(1, D), hbm),
        (out_heads.reshape(HD, D), hbm),
        (w_query_key.reshape(2 * D, 128), hbm),
        (w_value_gate.reshape(4 * D, 128), hbm),
        (w_beta_decay.transpose(1, 2, 0), hbm),
        (decay_scale, smem),
        (dt_bias, smem),
        (delta_gain.reshape(1, 128), hbm),
        (w_delta_out.reshape(2 * 128, D), hbm),
        (prior_state, hbm),
    )
    out = pl.pallas_call(
        kernel,
        out_shape=jax.ShapeDtypeStruct((ROWS, SHARE), f32),
        in_specs=[spec for _, spec in operands],
        out_specs=pl.BlockSpec(memory_space=pltpu.VMEM),
        scratch_shapes=[
            vmem((SLOTS, 2, PAGE, KVH * HD), f32),
            vmem((REQS, 1, PAGES), jnp.int32),
            vmem((REQS, 1, PAGES), jnp.int32),
            vmem((2, ROWS * GROUP, 128), f32),
            vmem((ROWS, GROUP, HD), bf16),
            vmem((ROWS, 2, KVH, HD), f32),
            vmem((REQS, STEPS, D), bf16),
            vmem((1, D), f32),
            vmem((HD, D), bf16),
            vmem((2 * D, 128), bf16),
            vmem((4 * D, 128), bf16),
            vmem((2, 2, D), bf16),
            vmem((1, 128), f32),
            vmem((2 * 128, D), bf16),
            vmem((REQS, GROUP, 2, 8, 128), f32),
            vmem((512, 128), f32),
            vmem((1024, 128), f32),
            vmem((D, 6 * 128), bf16),
            vmem((8, D), f32),
            vmem((GROUP, 64, 128), bf16),
            vmem((GROUP, 64, 128), bf16),
            vmem((GROUP, ROWS, MSG), bf16),
            vmem((GROUP - 1, ROWS, MSG), bf16),
            vmem((2, ROWS, D // 2), bf16),
            vmem((2, 3, ROWS, D // 2), bf16),
            vmem((2, ROWS, D // 2), bf16),
            vmem((2, 3, ROWS, D // 2), bf16),
            vmem((ROWS, D), f32),
            vmem((GROUP, ROWS, SHARE), bf16),
            vmem((GROUP - 1, ROWS, SHARE), bf16),
            pltpu.SemaphoreType.DMA((16,)),
            pltpu.SemaphoreType.DMA((8,)),
            pltpu.SemaphoreType.DMA((8,)),
            pltpu.SemaphoreType.REGULAR,
        ],
        compiler_params=pltpu.CompilerParams(
            collective_id=0, has_side_effects=True, vmem_limit_bytes=60 * 1024 * 1024
        ),
    )(*[value for value, _ in operands])
    return out.reshape(REQS, 1, STEPS, SHARE)


def solution(mesh):
    return jax.shard_map(
        body,
        mesh=mesh,
        in_specs=(
            P("req", "seq", None, None, None),
            P(None, "req", None),
            P(None, "req", None),
            P(None, "req"),
            P(None, "req", None, None, None),
            P(None, "req", None, None, None),
            P(None, "req", None, None, None, None),
            P(None, "req", None, None),
            P(),
            P("seq", None, None),
            P(None, "seq", None, None),
            P(None, "seq", None, None),
            P(None, None, "seq"),
            P("seq"),
            P("seq"),
            P(),
            P("seq", None, None),
            P(None, None, "req", "seq", None),
        ),
        out_specs=P(None, "req", None, "seq"),
        check_vma=False,
    )
```

```python
import jax
import jax.numpy as jnp
from jax import lax
from jax.experimental import pallas as pl
from jax.experimental.pallas import tpu as pltpu
from jax.sharding import PartitionSpec as P

floor_score = -1e30
norm_eps = 1e-06
MESH = pl.DeviceIdType.MESH
f32 = jnp.float32
bf16 = jnp.bfloat16

GROUP = 16
REQS = 4
STEPS = 4
ROWS = REQS * STEPS
BOTH = 2 * ROWS
LEVELS = 8
SLOTS = 48
PAGE = 16
TOKENS = SLOTS * PAGE
PAGES = 192
HD = 256
D = 2048
SHARE = 128
KVH = 2
PER_KV = 8
MSG = HD + 128
OFFSETS = [(y, x) for y in range(4) for x in range(4) if y or x]
FAR_FIRST = sorted(OFFSETS, key=lambda o: -(min(o[0], 4 - o[0]) + min(o[1], 4 - o[1])))
PLACES = (1, 0, 3, 2, 6, 5, 7, 4)


def dot(a, b):
    return jnp.dot(a, b, preferred_element_type=f32)


def dot_t(a, b):
    return lax.dot_general(a, b, (((1,), (1,)), ((), ())), preferred_element_type=f32)


def iota(shape, axis):
    return lax.broadcasted_iota(jnp.int32, shape, axis)


def shifted(x, by):
    return jnp.concatenate([x[-by:], x[:-by]], axis=0) if by else x


def kernel(
    kv_hbm, owner_hbm, slot_hbm, lengths, q_hbm, gates_hbm, new_hbm, tokens_hbm, gain_hbm, wo_hbm,
    wqk_hbm, wvg_hbm, wmix_hbm, decay_scale, dt_bias, dgain_hbm, wdo_hbm, state_hbm,
    out_ref,
    kv, owner, slot, q, gates, new, tokens, gain, wo, wqk, wvg, wmix, dgain, wdo, state,
    fq, fv, w_all, w_mix, s_out, s_more, s_in, held_states, m_out, m_in, draft_out, gate_out, gate_in,
    a_out, a_in, x_out, x_in, d_out, d_in, base_out, base_in,
    load_sem, send_sem, recv_sem, ready_sem, go_sem,
):
    i = lax.axis_index("req")
    me = lax.axis_index("seq")
    z = i // 2
    core = lax.rem(i, 2)
    front = 2 * z + 1
    back = 2 * z
    on_front = core == 1
    on_back = core == 0

    copies = {}

    def plan(name, src, dst):
        copies[name] = pltpu.make_async_copy(src, dst, load_sem.at[len(copies)])

    own_lanes = pl.ds(pl.multiple_of(me * SHARE, SHARE), SHARE)
    plan("q", q_hbm.at[:, 0:128], q.at[0])
    plan("q_more", q_hbm.at[:, 128:256], q.at[1])
    for k in range(KVH):
        for part in range(2):
            lanes = slice(k * HD, (k + 1) * HD)
            plan(("keys", "values")[part] + str(k), kv_hbm.at[:, part, :, lanes], kv.at[k, part])
    plan("owner", owner_hbm, owner)
    plan("slot", slot_hbm, slot)
    for copy in copies.values():
        copy.start()

    def rank(level):
        place = 0
        for n, p in enumerate(PLACES):
            place = jnp.where(level == n, p, place)
        return place

    def peer(offset):
        y, x = offset
        return lax.rem(me // 4 + y, 4) * 4 + lax.rem(lax.rem(me, 4) + x, 4)

    my_rank = rank(z)
    barrier = pltpu.get_barrier_semaphore()

    def greet(where):
        pl.semaphore_signal(barrier, inc=1, device_id=where, device_id_type=MESH)

    def each_state_source(use):
        for d in range(GROUP):
            use((2 * (me // 2), lax.rem(me + d, GROUP)))

    for offset in FAR_FIRST:
        greet((front, peer(offset)))

    @pl.when(on_back)
    def _():
        greet((front, me))

    @pl.when(on_front)
    def _():
        for offset in FAR_FIRST:
            greet((back, peer(offset)))
        greet((back, me))

    early_receiver = on_front & (my_rank <= rank(me // 2))
    late_receiver = on_front & (my_rank > rank(me // 2))

    @pl.when(early_receiver)
    def _():
        each_state_source(greet)

    for d in range(1, LEVELS):
        level = lax.rem(z + d, LEVELS)

        @pl.when(on_back & (rank(level) > my_rank))
        def _():
            for c in range(2):
                greet((2 * level + 1, 2 * z + c))

    copies["owner"].wait()
    copies["slot"].wait()
    page_at = iota((SLOTS, PAGES), 1)
    slot_at = iota((SLOTS, PAGES), 0)
    row_request = lax.rem(iota((SLOTS, 128), 1) // STEPS, REQS)
    counts = jnp.zeros((SLOTS, 128), f32)
    for r in range(REQS):
        live = jnp.clip(lengths[r] - page_at * PAGE, 0, PAGE)
        held = (owner[r] == me) & (slot[r] == slot_at)
        count = jnp.sum(jnp.where(held, live, 0).astype(f32), axis=1, keepdims=True)
        counts = jnp.where(row_request == r, count, counts)
    in_page = iota((SLOTS, PAGE, 128), 1).astype(f32)
    live_mask = (in_page < counts[:, None, :]).reshape(TOKENS, 128)

    def head_queries(h):
        halves = [q[half, pl.ds(h, ROWS, stride=GROUP), :] for half in range(2)]
        return jnp.concatenate(halves, axis=1) * (HD ** -0.5)

    def part_stats(top, total):
        lane = iota((top.shape[0], 128), 1)
        total_hi = total.astype(bf16).astype(f32)
        stats = jnp.where(lane == 0, top, jnp.where(lane == 1, total_hi, total - total_hi))
        return stats.astype(bf16)

    plan("state", state_hbm, state)
    plan("gates", gates_hbm, gates)
    plan("new", new_hbm, new)
    plan("wqk", wqk_hbm, wqk)
    plan("wvg", wvg_hbm, wvg)
    plan("wmix", wmix_hbm, wmix)
    plan("wo", wo_hbm, wo)
    plan("tokens", tokens_hbm.at[:, 0, :, own_lanes], tokens.at[1])
    plan("gain", gain_hbm, gain)
    plan("dgain", dgain_hbm, dgain)
    plan("wdo", wdo_hbm, wdo)

    copies["q"].wait()
    copies["q_more"].wait()
    for k in range(KVH):
        queries = jnp.concatenate([head_queries(k * PER_KV + h) for h in range(PER_KV)], axis=0)
        q_hi = queries.astype(bf16)
        q_lo = (queries - q_hi.astype(f32)).astype(bf16)
        copies["keys" + str(k)].wait()
        keys = kv[k, 0].reshape(TOKENS, HD)
        k_hi = keys.astype(bf16)
        k_lo = (keys - k_hi.astype(f32)).astype(bf16)
        by_hi = dot_t(k_hi, jnp.concatenate([q_hi, q_lo], axis=0))
        scores = by_hi[:, :128] + (by_hi[:, 128:] + dot_t(k_lo, q_hi))
        scores = jnp.where(live_mask, scores, floor_score)
        top = jnp.max(scores, axis=0, keepdims=True).astype(bf16).astype(f32)
        weights = jnp.where(live_mask, jnp.exp(scores - top), 0.0).astype(bf16)
        total = jnp.sum(weights.astype(f32), axis=0, keepdims=True)
        copies["values" + str(k)].wait()
        values = kv[k, 1].reshape(TOKENS, HD).astype(bf16)
        own = pl.ds(k * PER_KV, PER_KV)
        acc = lax.dot_general(weights, values, (((0,), (0,)), ((), ())), preferred_element_type=f32)
        m_out[own, :, 0:HD] = acc.astype(bf16).reshape(PER_KV, ROWS, HD)
        total_hi = total.astype(bf16).astype(f32)
        sides = jnp.concatenate([top, total_hi, total - total_hi, jnp.zeros((125, 128), f32)], axis=0)
        m_out[own, :, HD:MSG] = sides.T.astype(bf16).reshape(PER_KV, ROWS, 128)

    for name in ("state", "gates", "new"):
        copies[name].start()

    @pl.when(on_front)
    def _():
        for name in ("wqk", "wvg", "wmix", "wo", "tokens", "gain", "dgain", "wdo"):
            copies[name].start()

    pl.semaphore_wait(
        barrier,
        jnp.where(
            on_front,
            2 * GROUP - 1 + GROUP * late_receiver.astype(jnp.int32),
            GROUP + 2 * (my_rank + 1),
        ),
    )

    def send(src, dst, phase, where, sent_at=None):
        pltpu.make_async_remote_copy(
            src_ref=src,
            dst_ref=dst,
            send_sem=send_sem.at[phase if sent_at is None else sent_at],
            recv_sem=recv_sem.at[phase],
            device_id=where,
            device_id_type=MESH,
        ).start()

    def arrived(ref, phase):
        pltpu.make_async_copy(ref, ref, recv_sem.at[phase]).wait()

    def sent(ref, phase):
        pltpu.make_async_copy(ref, ref, send_sem.at[phase]).wait()

    for n, offset in enumerate(FAR_FIRST):
        other = peer(offset)
        send(m_out.at[other], m_in.at[n, core], 0, (front, other))

    @pl.when(on_back)
    def _():
        send(m_out.at[me], m_in.at[GROUP - 1, 0], 0, (front, me))
        send(tokens_hbm.at[:, 0, :, own_lanes], tokens.at[0], 9, (front, me))

    @pl.when(late_receiver)
    def _():
        each_state_source(
            lambda source: pl.semaphore_signal(
                ready_sem, inc=1, device_id=source, device_id_type=MESH
            )
        )

    copies["new"].wait()
    copies["gates"].wait()
    own_q = head_queries(me)
    low_kv = me < PER_KV

    def draft(component):
        both = new[:, component].astype(f32)
        return jnp.where(low_kv, both[:, 0], both[:, 1])

    draft_scores = lax.dot_general(
        own_q, draft(0), (((1,), (1,)), ((), ())),
        preferred_element_type=f32, precision=lax.Precision.HIGHEST,
    )
    row, col = iota((ROWS, ROWS), 0), iota((ROWS, ROWS), 1)
    causal = (row // STEPS == col // STEPS) & (col <= row)
    draft_scores = jnp.where(causal, draft_scores, floor_score)
    draft_top = jnp.max(draft_scores, axis=1, keepdims=True).astype(bf16).astype(f32)
    draft_weights = jnp.where(causal, jnp.exp(draft_scores - draft_top), 0.0)
    draft_acc = lax.dot_general(
        draft_weights, draft(1), (((1,), (0,)), ((), ())),
        preferred_element_type=f32, precision=lax.Precision.HIGHEST,
    )
    draft_out[:, 0:HD] = draft_acc.astype(bf16)
    draft_out[:, HD:MSG] = part_stats(draft_top, jnp.sum(draft_weights, axis=1, keepdims=True))
    own_gate = jnp.sum(
        jnp.where(iota((ROWS, GROUP, HD), 1) == me, gates[...].astype(f32), 0.0), axis=1
    )
    gate_out[...] = own_gate.astype(bf16)

    @pl.when(on_back)
    def _():
        send(draft_out, m_in.at[GROUP, 0], 0, (front, me))
        send(gate_out, gate_in, 8, (front, me))

    copies["state"].wait()
    for g in range(GROUP):
        s_out[g] = state[:, g].reshape(REQS * 2 * 8, 128).astype(bf16)

    @pl.when(on_back)
    def _():
        def send_states(c, chosen):
            for d in range(LEVELS):
                level = lax.rem(z + me + LEVELS - d, LEVELS)

                @pl.when(chosen(rank(level)))
                def _():
                    send(
                        (s_out, s_more)[c].at[pl.ds(2 * level, 2)], s_in.at[me], 1, (2 * level + 1, 2 * z + c)
                    )

        send_states(0, lambda place: place <= my_rank)
        arrived(s_more, 5)
        send_states(1, lambda place: place <= my_rank)

        @pl.when(my_rank < LEVELS - 1)
        def _():
            pl.semaphore_wait(ready_sem, 2 * (LEVELS - 1 - my_rank))

        pl.semaphore_wait(go_sem, 1)
        for c in range(2):
            send_states(c, lambda place: place > my_rank)
        sent(s_out, 1)
        sent(s_more, 1)

    @pl.when(on_front)
    def _():
        send(s_out, s_more, 5, (back, me))

    @pl.when(on_back)
    def _():
        sent(m_in.at[:, 0], 0)
        sent(tokens.at[0], 9)
        sent(gate_in, 8)
        arrived(base_in, 10)
        arrived(d_in, 4)
        result = base_in[...]
        for n in range(GROUP):
            result = result + d_in[n].astype(f32)
        out_ref[...] = result

    @pl.when(on_front)
    def _():
        m_in[GROUP - 1, 1] = m_out[me]
        m_in[GROUP, 1] = draft_out[...]

        copies["wqk"].wait()
        copies["wvg"].wait()
        chunk = 256

        def arrange(c, carry):
            rows = pl.ds(pl.multiple_of(c * chunk, chunk), chunk)
            fq[...] = wqk[pl.ds(pl.multiple_of(c * (2 * chunk), 2 * chunk), 2 * chunk), :].astype(f32)
            fv[...] = wvg[pl.ds(pl.multiple_of(c * (4 * chunk), 4 * chunk), 4 * chunk), :].astype(f32)
            for n in range(2):
                w_all[rows, n * 128 : (n + 1) * 128] = fq[pl.ds(n, chunk, stride=2), :].astype(bf16)
            for n in range(4):
                w_all[rows, (n + 2) * 128 : (n + 3) * 128] = fv[pl.ds(n, chunk, stride=4), :].astype(bf16)
            return carry

        lax.fori_loop(0, D // chunk, arrange, 0)
        copies["wmix"].wait()
        for n in range(2):
            w_mix[2 * n : 2 * n + 2, :] = wmix[n].astype(f32)
        for name in ("wo", "tokens", "gain", "dgain", "wdo"):
            copies[name].wait()
        arrived(gate_in, 8)
        arrived(tokens.at[0], 9)
        gate = jax.nn.sigmoid(jnp.concatenate([gate_in[...], gate_out[...]], axis=0).astype(f32))

        arrived(m_in.at[pl.ds(0, GROUP)], 0)
        pl.semaphore_signal(go_sem, inc=1, device_id=(back, me), device_id_type=MESH)
        parts = [m_in[n].reshape(BOTH, MSG) for n in range(GROUP + 1)]
        ceiling = parts[0][:, HD : HD + 1].astype(f32)
        for part in parts[1:]:
            ceiling = jnp.maximum(ceiling, part[:, HD : HD + 1].astype(f32))
        total = jnp.zeros((BOTH, 1), f32)
        acc = jnp.zeros((BOTH, HD), f32)
        for part in parts:
            stats = part[:, HD:MSG].astype(f32)
            factor = jnp.exp(stats[:, 0:1] - ceiling)
            total = total + factor * (stats[:, 1:2] + stats[:, 2:3])
            acc = acc + factor * part[:, 0:HD].astype(f32)
        gated = (acc / total * gate).astype(bf16)

        total = dot(gated, wo[...])
        for e in range(GROUP):
            a_out[e] = total[:, e * SHARE : (e + 1) * SHARE].astype(bf16)
        for n, offset in enumerate(FAR_FIRST):
            other = peer(offset)
            send(a_out.at[other], a_in.at[n], 2, (front, other))
        stream = tokens[...].astype(f32).reshape(BOTH, SHARE) + a_out[me].astype(f32)
        arrived(a_in, 2)
        for n in range(GROUP - 1):
            stream = stream + a_in[n].astype(f32)

        own_x = (stream * gain[:, own_lanes]).astype(bf16)
        x_out[...] = own_x
        x_in[me] = own_x
        for offset in FAR_FIRST:
            send(x_out, x_in.at[me], 3, (front, peer(offset)))
        base_out[...] = stream[0:ROWS]
        send(base_out, base_in, 10, (back, me))

        arrived(s_in, 1)
        for g in range(2):
            for r in range(REQS):
                rows = s_in[:, g, r * 16 : (r + 1) * 16].astype(f32).reshape(GROUP, 2, 8, 128)
                blocks = [rows[j, h] for h in range(2) for j in range(GROUP)]
                held_states[g * REQS + r] = jnp.concatenate(blocks, axis=0).astype(bf16)

        arrived(x_in.at[pl.ds(0, GROUP - 1)], 3)
        y = jnp.concatenate([x_in[e] for e in range(GROUP)], axis=1)
        proj = dot(y, w_all[...])
        y = y.astype(f32)
        mixes = [jnp.sum(y * w_mix[c : c + 1], axis=1, keepdims=True) for c in range(4)]
        x = y / gain[...]
        squares = jnp.sum(x * x, axis=1, keepdims=True)
        scale = lax.rsqrt(squares * (1.0 / D) + norm_eps)
        proj = proj * scale
        mixes = [mix * scale for mix in mixes]

        def unit(x):
            return x * lax.rsqrt(jnp.sum(x * x, axis=1, keepdims=True) + norm_eps)

        dq = unit(proj[:, 0:128])
        dk = unit(proj[:, 128:256])
        value = jnp.concatenate([proj[:, 256:384], proj[:, 512:640]], axis=1)
        zgate = jnp.concatenate([proj[:, 384:512], proj[:, 640:768]], axis=1)
        wide = (BOTH, 2 * 128)
        high = iota(wide, 1) >= 128
        beta = jnp.where(high, jax.nn.sigmoid(mixes[1]), jax.nn.sigmoid(mixes[0]))

        def decay_of(h):
            t = mixes[2 + h] + dt_bias[h]
            soft = jnp.maximum(t, 0.0) + jnp.log(1.0 + jnp.exp(-jnp.abs(t)))
            return jnp.exp(-decay_scale[h] * soft)

        decay = jnp.where(high, decay_of(1), decay_of(0))

        both = jnp.concatenate([dk, dq], axis=0).astype(bf16)
        row_of = lax.rem(iota((2 * BOTH, 2 * 128), 0) // STEPS, 2 * REQS)
        prior = jnp.zeros((2 * BOTH, 2 * 128), f32)
        for r in range(2 * REQS):
            prior = jnp.where(row_of == r, dot_t(both, held_states[r]), prior)
        prior_k, prior_q = prior[:BOTH], prior[BOTH:]
        step = lax.rem(iota(wide, 0), STEPS)
        ratio = [jnp.ones(wide, f32), decay]
        for o in range(1, STEPS):
            ratio.append(decay * shifted(ratio[o], 1))
        whole = jnp.where(
            step == 0, ratio[1], jnp.where(step == 1, ratio[2], jnp.where(step == 2, ratio[3], ratio[4]))
        )
        key_back = [shifted(dk, o) for o in range(STEPS)]
        beta_prior = beta * (value - whole * prior_k)
        coupling = [
            jnp.where(step >= o, beta * ratio[o] * jnp.sum(dk * key_back[o], axis=1, keepdims=True), 0.0)
            for o in range(1, STEPS)
        ]
        update = beta_prior
        for _ in range(STEPS - 1):
            following = beta_prior
            for o in range(1, STEPS):
                following = following - coupling[o - 1] * shifted(update, o)
            update = following
        readout = whole * prior_q
        for o in range(STEPS):
            reach = jnp.sum(dq * key_back[o], axis=1, keepdims=True)
            readout = readout + jnp.where(step >= o, ratio[o] * reach, 0.0) * shifted(update, o)
        readout = readout * (128 ** -0.5)

        def normal(x):
            return x * lax.rsqrt(jnp.mean(x * x, axis=1, keepdims=True) + norm_eps) * dgain[...]

        normalized = jnp.concatenate([normal(readout[:, :128]), normal(readout[:, 128:])], axis=1)
        normalized = (normalized * zgate * jax.nn.sigmoid(zgate)).astype(bf16)

        total = dot(normalized, wdo[...])
        for e in range(GROUP):
            d_out[:, e] = total[:, e * SHARE : (e + 1) * SHARE].astype(bf16).reshape(2, ROWS, SHARE)
        for n, offset in enumerate(FAR_FIRST):
            other = peer(offset)
            send(d_out.at[0, other], d_in.at[n], 4, (back, other))
            send(d_out.at[1, other], d_in.at[n], 4, (front, other))
        send(d_out.at[0, me], d_in.at[GROUP - 1], 4, (back, me))
        result = stream[ROWS:BOTH] + d_out[1, me].astype(f32)
        sent(m_in.at[pl.ds(0, GROUP - 1), 0], 0)
        sent(s_more, 5)
        sent(a_in, 2)
        sent(x_in.at[pl.ds(0, GROUP - 1)], 3)
        sent(base_out, 10)
        arrived(d_in.at[pl.ds(0, GROUP - 1)], 4)
        for n in range(GROUP - 1):
            result = result + d_in[n].astype(f32)
        out_ref[...] = result
        sent(d_out.at[0], 4)
        sent(d_out.at[1, pl.ds(0, GROUP - 1)], 4)


def body(
    kv_pool, page_owner, page_slot, lengths, queries, gates, new_kv, tokens, attn_gain, out_heads,
    w_query_key, w_value_gate, w_beta_decay, decay_scale, dt_bias, delta_gain, w_delta_out, prior_state,
):
    hbm = pl.BlockSpec(memory_space=pl.ANY)
    smem = pl.BlockSpec(memory_space=pltpu.SMEM)
    vmem = pltpu.VMEM
    operands = (
        (kv_pool.reshape(SLOTS, 2, PAGE, KVH * HD), hbm),
        (page_owner, hbm),
        (page_slot, hbm),
        (lengths.reshape(REQS), smem),
        (queries.reshape(ROWS * GROUP, HD), hbm),
        (gates.reshape(ROWS, GROUP, HD), hbm),
        (new_kv.reshape(ROWS, 2, KVH, HD), hbm),
        (tokens, hbm),
        (attn_gain.reshape(1, D), hbm),
        (out_heads.reshape(HD, D), hbm),
        (w_query_key.reshape(2 * D, 128), hbm),
        (w_value_gate.reshape(4 * D, 128), hbm),
        (w_beta_decay.transpose(1, 2, 0), hbm),
        (decay_scale, smem),
        (dt_bias, smem),
        (delta_gain.reshape(1, 128), hbm),
        (w_delta_out.reshape(2 * 128, D), hbm),
        (prior_state, hbm),
    )
    out = pl.pallas_call(
        kernel,
        out_shape=jax.ShapeDtypeStruct((ROWS, SHARE), f32),
        in_specs=[spec for _, spec in operands],
        out_specs=pl.BlockSpec(memory_space=pltpu.VMEM),
        scratch_shapes=[
            vmem((KVH, 2, SLOTS, PAGE, HD), f32),
            vmem((REQS, 1, PAGES), jnp.int32),
            vmem((REQS, 1, PAGES), jnp.int32),
            vmem((2, ROWS * GROUP, 128), f32),
            vmem((ROWS, GROUP, HD), bf16),
            vmem((ROWS, 2, KVH, HD), f32),
            vmem((2, REQS, STEPS, SHARE), bf16),
            vmem((1, D), f32),
            vmem((HD, D), bf16),
            vmem((2 * D, 128), bf16),
            vmem((4 * D, 128), bf16),
            vmem((2, 2, D), bf16),
            vmem((1, 128), f32),
            vmem((2 * 128, D), bf16),
            vmem((REQS, GROUP, 2, 8, 128), f32),
            vmem((512, 128), f32),
            vmem((1024, 128), f32),
            vmem((D, 6 * 128), bf16),
            vmem((8, D), f32),
            vmem((GROUP, 64, 128), bf16),
            vmem((GROUP, 64, 128), bf16),
            vmem((GROUP, 2, 64, 128), bf16),
            vmem((2 * REQS, 256, 128), bf16),
            vmem((GROUP, ROWS, MSG), bf16),
            vmem((GROUP + 1, 2, ROWS, MSG), bf16),
            vmem((ROWS, MSG), bf16),
            vmem((ROWS, HD), bf16),
            vmem((ROWS, HD), bf16),
            vmem((GROUP, BOTH, SHARE), bf16),
            vmem((GROUP - 1, BOTH, SHARE), bf16),
            vmem((BOTH, SHARE), bf16),
            vmem((GROUP, BOTH, SHARE), bf16),
            vmem((2, GROUP, ROWS, SHARE), bf16),
            vmem((GROUP, ROWS, SHARE), bf16),
            vmem((ROWS, SHARE), f32),
            vmem((ROWS, SHARE), f32),
            pltpu.SemaphoreType.DMA((20,)),
            pltpu.SemaphoreType.DMA((11,)),
            pltpu.SemaphoreType.DMA((11,)),
            pltpu.SemaphoreType.REGULAR,
            pltpu.SemaphoreType.REGULAR,
        ],
        compiler_params=pltpu.CompilerParams(
            collective_id=0, has_side_effects=True, vmem_limit_bytes=60 * 1024 * 1024
        ),
    )(*[value for value, _ in operands])
    return out.reshape(REQS, 1, STEPS, SHARE)


def solution(mesh):
    return jax.shard_map(
        body,
        mesh=mesh,
        in_specs=(
            P("req", "seq", None, None, None),
            P(None, "req", None),
            P(None, "req", None),
            P(None, "req"),
            P(None, "req", None, None, None),
            P(None, "req", None, None, None),
            P(None, "req", None, None, None, None),
            P(None, "req", None, None),
            P(),
            P("seq", None, None),
            P(None, "seq", None, None),
            P(None, "seq", None, None),
            P(None, None, "seq"),
            P("seq"),
            P("seq"),
            P(),
            P("seq", None, None),
            P(None, None, "req", "seq", None),
        ),
        out_specs=P(None, "req", None, "seq"),
        check_vma=False,
    )
```

```python
import jax
import jax.numpy as jnp
from jax import lax
from jax.experimental import pallas as pl
from jax.experimental.pallas import tpu as pltpu
from jax.sharding import PartitionSpec as P

floor_score = -1e30
norm_eps = 1e-06
MESH = pl.DeviceIdType.MESH
f32 = jnp.float32
bf16 = jnp.bfloat16

GROUP = 16
REQS = 4
STEPS = 4
ROWS = REQS * STEPS
BOTH = 2 * ROWS
LEVELS = 8
SLOTS = 48
PAGE = 16
TOKENS = SLOTS * PAGE
PAGES = 192
HD = 256
D = 2048
SHARE = 128
KVH = 2
PER_KV = 8
MSG = HD + 128
OFFSETS = [(y, x) for y in range(4) for x in range(4) if y or x]
FAR_FIRST = sorted(OFFSETS, key=lambda o: -(min(o[0], 4 - o[0]) + min(o[1], 4 - o[1])))
PLACES = (1, 0, 3, 2, 6, 5, 7, 4)
ORDER = (1, 0, 3, 2, 7, 5, 4, 6)


def dot(a, b):
    return jnp.dot(a, b, preferred_element_type=f32)


def dot_t(a, b):
    return lax.dot_general(a, b, (((1,), (1,)), ((), ())), preferred_element_type=f32)


def iota(shape, axis):
    return lax.broadcasted_iota(jnp.int32, shape, axis)


def shifted(x, by):
    return jnp.concatenate([x[-by:], x[:-by]], axis=0) if by else x


def kernel(
    kv_hbm, owner_hbm, slot_hbm, lengths, q_hbm, gates_hbm, new_hbm, tokens_hbm, gain_hbm, wo_hbm,
    wqk_hbm, wvg_hbm, wmix_hbm, decay_scale, dt_bias, dgain_hbm, wdo_hbm, state_hbm,
    out_ref,
    kv, owner, slot, q, gates, new, tokens, gain, wo, wqk, wvg, wmix, dgain, wdo, state,
    fq, fv, w_all, w_mix, s_out, s_more, s_in, held_states, m_out, m_in, draft_out, gate_out, gate_in,
    a_out, a_in, x_out, x_in, d_out, d_in, base_out, base_in,
    load_sem, send_sem, recv_sem, ready_sem,
):
    i = lax.axis_index("req")
    me = lax.axis_index("seq")
    z = i // 2
    core = lax.rem(i, 2)
    front = 2 * z + 1
    back = 2 * z
    on_front = core == 1
    on_back = core == 0

    copies = {}

    def plan(name, src, dst):
        copies[name] = pltpu.make_async_copy(src, dst, load_sem.at[len(copies)])

    own_lanes = pl.ds(pl.multiple_of(me * SHARE, SHARE), SHARE)
    plan("q", q_hbm.at[:, 0:128], q.at[0])
    plan("q_more", q_hbm.at[:, 128:256], q.at[1])
    for k in range(KVH):
        for part in range(2):
            lanes = slice(k * HD, (k + 1) * HD)
            plan(("keys", "values")[part] + str(k), kv_hbm.at[:, part, :, lanes], kv.at[k, part])
    plan("owner", owner_hbm, owner)
    plan("slot", slot_hbm, slot)
    for copy in copies.values():
        copy.start()

    def rank(level):
        place = 0
        for n, p in enumerate(PLACES):
            place = jnp.where(level == n, p, place)
        return place

    def peer(offset):
        y, x = offset
        return lax.rem(me // 4 + y, 4) * 4 + lax.rem(lax.rem(me, 4) + x, 4)

    my_rank = rank(z)
    barrier = pltpu.get_barrier_semaphore()

    def greet(where):
        pl.semaphore_signal(barrier, inc=1, device_id=where, device_id_type=MESH)

    def each_state_source(use):
        for d in range(GROUP):
            use((2 * (me // 2), lax.rem(me + d, GROUP)))

    @pl.when(on_back)
    def _():
        greet((front, me))

    @pl.when(on_front)
    def _():
        for offset in FAR_FIRST:
            greet((back, peer(offset)))
            greet((front, peer(offset)))
        greet((back, me))

    early_receiver = on_front & (my_rank < rank(me // 2))
    own_receiver = on_front & (z == me // 2)
    late_receiver = on_front & (my_rank > rank(me // 2))

    @pl.when(early_receiver)
    def _():
        for d in range(GROUP):
            greet((me, lax.rem(me + d, GROUP)))

    @pl.when(own_receiver)
    def _():
        each_state_source(greet)

    for d in range(1, LEVELS):
        level = lax.rem(z + d, LEVELS)

        @pl.when(on_back & (rank(level) > my_rank))
        def _():
            for c in range(2):
                greet((2 * level + 1, 2 * z + c))

    copies["owner"].wait()
    copies["slot"].wait()
    page_at = iota((SLOTS, PAGES), 1)
    slot_at = iota((SLOTS, PAGES), 0)
    row_request = lax.rem(iota((SLOTS, 128), 1) // STEPS, REQS)
    counts = jnp.zeros((SLOTS, 128), f32)
    for r in range(REQS):
        live = jnp.clip(lengths[r] - page_at * PAGE, 0, PAGE)
        held = (owner[r] == me) & (slot[r] == slot_at)
        count = jnp.sum(jnp.where(held, live, 0).astype(f32), axis=1, keepdims=True)
        counts = jnp.where(row_request == r, count, counts)
    in_page = iota((SLOTS, PAGE, 128), 1).astype(f32)
    live_mask = (in_page < counts[:, None, :]).reshape(TOKENS, 128)

    def head_queries(h):
        halves = [q[half, pl.ds(h, ROWS, stride=GROUP), :] for half in range(2)]
        return jnp.concatenate(halves, axis=1) * (HD ** -0.5)

    def part_stats(top, total):
        lane = iota((top.shape[0], 128), 1)
        total_hi = total.astype(bf16).astype(f32)
        stats = jnp.where(lane == 0, top, jnp.where(lane == 1, total_hi, total - total_hi))
        return stats.astype(bf16)

    plan("state", state_hbm, state)
    plan("gates", gates_hbm, gates)
    plan("new", new_hbm, new)
    plan("wqk", wqk_hbm, wqk)
    plan("wvg", wvg_hbm, wvg)
    plan("wmix", wmix_hbm, wmix)
    plan("wo", wo_hbm, wo)
    plan("tokens", tokens_hbm.at[:, 0, :, own_lanes], tokens.at[1])
    plan("gain", gain_hbm, gain)
    plan("dgain", dgain_hbm, dgain)
    plan("wdo", wdo_hbm, wdo)

    copies["q"].wait()
    copies["q_more"].wait()
    for k in range(KVH):
        queries = jnp.concatenate([head_queries(k * PER_KV + h) for h in range(PER_KV)], axis=0)
        q_hi = queries.astype(bf16)
        q_lo = (queries - q_hi.astype(f32)).astype(bf16)
        copies["keys" + str(k)].wait()
        keys = kv[k, 0].reshape(TOKENS, HD)
        k_hi = keys.astype(bf16)
        k_lo = (keys - k_hi.astype(f32)).astype(bf16)
        by_hi = dot_t(k_hi, jnp.concatenate([q_hi, q_lo], axis=0))
        scores = by_hi[:, :128] + (by_hi[:, 128:] + dot_t(k_lo, q_hi))
        scores = jnp.where(live_mask, scores, floor_score)
        top = jnp.max(scores, axis=0, keepdims=True).astype(bf16).astype(f32)
        weights = jnp.where(live_mask, jnp.exp(scores - top), 0.0).astype(bf16)
        total = jnp.sum(weights.astype(f32), axis=0, keepdims=True)
        copies["values" + str(k)].wait()
        values = kv[k, 1].reshape(TOKENS, HD).astype(bf16)
        own = pl.ds(k * PER_KV, PER_KV)
        acc = lax.dot_general(weights, values, (((0,), (0,)), ((), ())), preferred_element_type=f32)
        m_out[own, :, 0:HD] = acc.astype(bf16).reshape(PER_KV, ROWS, HD)
        total_hi = total.astype(bf16).astype(f32)
        sides = jnp.concatenate([top, total_hi, total - total_hi, jnp.zeros((125, 128), f32)], axis=0)
        m_out[own, :, HD:MSG] = sides.T.astype(bf16).reshape(PER_KV, ROWS, 128)

    for name in ("state", "gates", "new"):
        copies[name].start()

    @pl.when(on_front)
    def _():
        for name in ("wqk", "wvg", "wmix", "wo", "tokens", "gain", "dgain", "wdo"):
            copies[name].start()

    pl.semaphore_wait(
        barrier,
        jnp.where(
            on_front,
            GROUP + my_rank + GROUP * late_receiver.astype(jnp.int32),
            GROUP + my_rank + 2,
        ),
    )

    def send(src, dst, phase, where, sent_at=None):
        pltpu.make_async_remote_copy(
            src_ref=src,
            dst_ref=dst,
            send_sem=send_sem.at[phase if sent_at is None else sent_at],
            recv_sem=recv_sem.at[phase],
            device_id=where,
            device_id_type=MESH,
        ).start()

    def arrived(ref, phase):
        pltpu.make_async_copy(ref, ref, recv_sem.at[phase]).wait()

    def sent(ref, phase):
        pltpu.make_async_copy(ref, ref, send_sem.at[phase]).wait()

    for n, offset in enumerate(FAR_FIRST):
        other = peer(offset)
        send(m_out.at[other], m_in.at[n, core], 0, (front, other))

    @pl.when(on_back)
    def _():
        send(m_out.at[me], m_in.at[GROUP - 1, 0], 0, (front, me))
        send(tokens_hbm.at[:, 0, :, own_lanes], tokens.at[0], 9, (front, me))

    @pl.when(late_receiver)
    def _():
        each_state_source(
            lambda source: pl.semaphore_signal(
                ready_sem.at[z], inc=1, device_id=source, device_id_type=MESH
            )
        )

    copies["new"].wait()
    copies["gates"].wait()
    own_q = head_queries(me)
    low_kv = me < PER_KV

    def draft(component):
        both = new[:, component].astype(f32)
        return jnp.where(low_kv, both[:, 0], both[:, 1])

    draft_scores = lax.dot_general(
        own_q, draft(0), (((1,), (1,)), ((), ())),
        preferred_element_type=f32, precision=lax.Precision.HIGHEST,
    )
    row, col = iota((ROWS, ROWS), 0), iota((ROWS, ROWS), 1)
    causal = (row // STEPS == col // STEPS) & (col <= row)
    draft_scores = jnp.where(causal, draft_scores, floor_score)
    draft_top = jnp.max(draft_scores, axis=1, keepdims=True).astype(bf16).astype(f32)
    draft_weights = jnp.where(causal, jnp.exp(draft_scores - draft_top), 0.0)
    draft_acc = lax.dot_general(
        draft_weights, draft(1), (((1,), (0,)), ((), ())),
        preferred_element_type=f32, precision=lax.Precision.HIGHEST,
    )
    draft_out[:, 0:HD] = draft_acc.astype(bf16)
    draft_out[:, HD:MSG] = part_stats(draft_top, jnp.sum(draft_weights, axis=1, keepdims=True))
    own_gate = jnp.sum(
        jnp.where(iota((ROWS, GROUP, HD), 1) == me, gates[...].astype(f32), 0.0), axis=1
    )
    gate_out[...] = own_gate.astype(bf16)

    @pl.when(on_back)
    def _():
        send(draft_out, m_in.at[GROUP, 0], 0, (front, me))
        send(gate_out, gate_in, 8, (front, me))

    copies["state"].wait()
    for g in range(GROUP):
        s_out[g] = state[:, g].reshape(REQS * 2 * 8, 128).astype(bf16)

    def send_states(src, c, phase_sent, chosen):
        for d in range(LEVELS):
            level = lax.rem(z + me + LEVELS - d, LEVELS)

            @pl.when(chosen(rank(level)))
            def _():
                send(src.at[pl.ds(2 * level, 2)], s_in.at[me], 1, (2 * level + 1, 2 * z + c), phase_sent)

    @pl.when(on_back)
    def _():
        send_states(s_out, 0, 1, lambda place: place <= my_rank)
        arrived(s_more, 5)
        send_states(s_more, 1, 6, lambda place: place == my_rank)

        for r, level in enumerate(ORDER):
            @pl.when(my_rank < r)
            def _():
                pl.semaphore_wait(ready_sem.at[level], 2)
                for c in range(2):
                    send(
                        (s_out, s_more)[c].at[pl.ds(2 * level, 2)], s_in.at[me], 1, (2 * level + 1, 2 * z + c), (1, 6)[c]
                    )

        sent(s_out, 1)
        for r in range(LEVELS):

            @pl.when(my_rank == r)
            def _():
                sent(s_more.at[pl.ds(0, 2 * (LEVELS - r))], 6)

    @pl.when(on_front)
    def _():
        send_states(s_out, 1, 1, lambda place: place < my_rank)
        send(s_out, s_more, 5, (back, me))

    @pl.when(on_back)
    def _():
        sent(m_in.at[:, 0], 0)
        sent(tokens.at[0], 9)
        sent(gate_in, 8)
        arrived(base_in, 10)
        arrived(d_in, 4)
        result = base_in[...]
        for n in range(GROUP):
            result = result + d_in[n].astype(f32)
        out_ref[...] = result

    @pl.when(on_front)
    def _():
        m_in[GROUP - 1, 1] = m_out[me]
        m_in[GROUP, 1] = draft_out[...]

        copies["wqk"].wait()
        copies["wvg"].wait()
        chunk = 256

        def arrange(c, carry):
            rows = pl.ds(pl.multiple_of(c * chunk, chunk), chunk)
            fq[...] = wqk[pl.ds(pl.multiple_of(c * (2 * chunk), 2 * chunk), 2 * chunk), :].astype(f32)
            fv[...] = wvg[pl.ds(pl.multiple_of(c * (4 * chunk), 4 * chunk), 4 * chunk), :].astype(f32)
            for n in range(2):
                w_all[rows, n * 128 : (n + 1) * 128] = fq[pl.ds(n, chunk, stride=2), :].astype(bf16)
            for n in range(4):
                w_all[rows, (n + 2) * 128 : (n + 3) * 128] = fv[pl.ds(n, chunk, stride=4), :].astype(bf16)
            return carry

        lax.fori_loop(0, D // chunk, arrange, 0)
        copies["wmix"].wait()
        for n in range(2):
            w_mix[2 * n : 2 * n + 2, :] = wmix[n].astype(f32)
        for name in ("wo", "tokens", "gain", "dgain", "wdo"):
            copies[name].wait()
        arrived(gate_in, 8)
        arrived(tokens.at[0], 9)
        gate = jax.nn.sigmoid(jnp.concatenate([gate_in[...], gate_out[...]], axis=0).astype(f32))

        arrived(m_in.at[pl.ds(0, GROUP)], 0)
        parts = [m_in[n].reshape(BOTH, MSG) for n in range(GROUP + 1)]
        ceiling = parts[0][:, HD : HD + 1].astype(f32)
        for part in parts[1:]:
            ceiling = jnp.maximum(ceiling, part[:, HD : HD + 1].astype(f32))
        total = jnp.zeros((BOTH, 1), f32)
        acc = jnp.zeros((BOTH, HD), f32)
        for part in parts:
            stats = part[:, HD:MSG].astype(f32)
            factor = jnp.exp(stats[:, 0:1] - ceiling)
            total = total + factor * (stats[:, 1:2] + stats[:, 2:3])
            acc = acc + factor * part[:, 0:HD].astype(f32)
        gated = (acc / total * gate).astype(bf16)

        total = dot(gated, wo[...])
        for e in range(GROUP):
            a_out[e] = total[:, e * SHARE : (e + 1) * SHARE].astype(bf16)
        for n, offset in enumerate(FAR_FIRST):
            other = peer(offset)
            send(a_out.at[other], a_in.at[n], 2, (front, other))
        stream = tokens[...].astype(f32).reshape(BOTH, SHARE) + a_out[me].astype(f32)
        arrived(a_in, 2)
        for n in range(GROUP - 1):
            stream = stream + a_in[n].astype(f32)

        own_x = (stream * gain[:, own_lanes]).astype(bf16)
        x_out[...] = own_x
        x_in[me] = own_x
        for offset in FAR_FIRST:
            send(x_out, x_in.at[me], 3, (front, peer(offset)))
        base_out[...] = stream[0:ROWS]
        send(base_out, base_in, 10, (back, me))

        arrived(s_in, 1)
        for g in range(2):
            for r in range(REQS):
                rows = s_in[:, g, r * 16 : (r + 1) * 16].astype(f32).reshape(GROUP, 2, 8, 128)
                blocks = [rows[j, h] for h in range(2) for j in range(GROUP)]
                held_states[g * REQS + r] = jnp.concatenate(blocks, axis=0).astype(bf16)

        arrived(x_in.at[pl.ds(0, GROUP - 1)], 3)
        y = jnp.concatenate([x_in[e] for e in range(GROUP)], axis=1)
        proj = dot(y, w_all[...])
        y = y.astype(f32)
        mixes = [jnp.sum(y * w_mix[c : c + 1], axis=1, keepdims=True) for c in range(4)]
        x = y / gain[...]
        squares = jnp.sum(x * x, axis=1, keepdims=True)
        scale = lax.rsqrt(squares * (1.0 / D) + norm_eps)
        proj = proj * scale
        mixes = [mix * scale for mix in mixes]

        def unit(x):
            return x * lax.rsqrt(jnp.sum(x * x, axis=1, keepdims=True) + norm_eps)

        dq = unit(proj[:, 0:128])
        dk = unit(proj[:, 128:256])
        value = jnp.concatenate([proj[:, 256:384], proj[:, 512:640]], axis=1)
        zgate = jnp.concatenate([proj[:, 384:512], proj[:, 640:768]], axis=1)
        wide = (BOTH, 2 * 128)
        high = iota(wide, 1) >= 128
        beta = jnp.where(high, jax.nn.sigmoid(mixes[1]), jax.nn.sigmoid(mixes[0]))

        def decay_of(h):
            t = mixes[2 + h] + dt_bias[h]
            soft = jnp.maximum(t, 0.0) + jnp.log(1.0 + jnp.exp(-jnp.abs(t)))
            return jnp.exp(-decay_scale[h] * soft)

        decay = jnp.where(high, decay_of(1), decay_of(0))

        both = jnp.concatenate([dk, dq], axis=0).astype(bf16)
        row_of = lax.rem(iota((2 * BOTH, 2 * 128), 0) // STEPS, 2 * REQS)
        prior = jnp.zeros((2 * BOTH, 2 * 128), f32)
        for r in range(2 * REQS):
            prior = jnp.where(row_of == r, dot_t(both, held_states[r]), prior)
        prior_k, prior_q = prior[:BOTH], prior[BOTH:]
        step = lax.rem(iota(wide, 0), STEPS)
        ratio = [jnp.ones(wide, f32), decay]
        for o in range(1, STEPS):
            ratio.append(decay * shifted(ratio[o], 1))
        whole = jnp.where(
            step == 0, ratio[1], jnp.where(step == 1, ratio[2], jnp.where(step == 2, ratio[3], ratio[4]))
        )
        key_back = [shifted(dk, o) for o in range(STEPS)]
        beta_prior = beta * (value - whole * prior_k)
        coupling = [
            jnp.where(step >= o, beta * ratio[o] * jnp.sum(dk * key_back[o], axis=1, keepdims=True), 0.0)
            for o in range(1, STEPS)
        ]
        update = beta_prior
        for _ in range(STEPS - 1):
            following = beta_prior
            for o in range(1, STEPS):
                following = following - coupling[o - 1] * shifted(update, o)
            update = following
        readout = whole * prior_q
        for o in range(STEPS):
            reach = jnp.sum(dq * key_back[o], axis=1, keepdims=True)
            readout = readout + jnp.where(step >= o, ratio[o] * reach, 0.0) * shifted(update, o)
        readout = readout * (128 ** -0.5)

        def normal(x):
            return x * lax.rsqrt(jnp.mean(x * x, axis=1, keepdims=True) + norm_eps) * dgain[...]

        normalized = jnp.concatenate([normal(readout[:, :128]), normal(readout[:, 128:])], axis=1)
        normalized = (normalized * zgate * jax.nn.sigmoid(zgate)).astype(bf16)

        total = dot(normalized, wdo[...])
        for e in range(GROUP):
            d_out[:, e] = total[:, e * SHARE : (e + 1) * SHARE].astype(bf16).reshape(2, ROWS, SHARE)
        for n, offset in enumerate(FAR_FIRST):
            other = peer(offset)
            send(d_out.at[0, other], d_in.at[n], 4, (back, other))
            send(d_out.at[1, other], d_in.at[n], 4, (front, other))
        send(d_out.at[0, me], d_in.at[GROUP - 1], 4, (back, me))
        result = stream[ROWS:BOTH] + d_out[1, me].astype(f32)
        sent(m_in.at[pl.ds(0, GROUP - 1), 0], 0)
        sent(s_more, 5)
        for r in range(1, LEVELS):

            @pl.when(my_rank == r)
            def _():
                sent(s_out.at[pl.ds(0, 2 * r)], 1)

        sent(a_in, 2)
        sent(x_in.at[pl.ds(0, GROUP - 1)], 3)
        sent(base_out, 10)
        arrived(d_in.at[pl.ds(0, GROUP - 1)], 4)
        for n in range(GROUP - 1):
            result = result + d_in[n].astype(f32)
        out_ref[...] = result
        sent(d_out.at[0], 4)
        sent(d_out.at[1, pl.ds(0, GROUP - 1)], 4)


def body(
    kv_pool, page_owner, page_slot, lengths, queries, gates, new_kv, tokens, attn_gain, out_heads,
    w_query_key, w_value_gate, w_beta_decay, decay_scale, dt_bias, delta_gain, w_delta_out, prior_state,
):
    hbm = pl.BlockSpec(memory_space=pl.ANY)
    smem = pl.BlockSpec(memory_space=pltpu.SMEM)
    vmem = pltpu.VMEM
    operands = (
        (kv_pool.reshape(SLOTS, 2, PAGE, KVH * HD), hbm),
        (page_owner, hbm),
        (page_slot, hbm),
        (lengths.reshape(REQS), smem),
        (queries.reshape(ROWS * GROUP, HD), hbm),
        (gates.reshape(ROWS, GROUP, HD), hbm),
        (new_kv.reshape(ROWS, 2, KVH, HD), hbm),
        (tokens, hbm),
        (attn_gain.reshape(1, D), hbm),
        (out_heads.reshape(HD, D), hbm),
        (w_query_key.reshape(2 * D, 128), hbm),
        (w_value_gate.reshape(4 * D, 128), hbm),
        (w_beta_decay.transpose(1, 2, 0), hbm),
        (decay_scale, smem),
        (dt_bias, smem),
        (delta_gain.reshape(1, 128), hbm),
        (w_delta_out.reshape(2 * 128, D), hbm),
        (prior_state, hbm),
    )
    out = pl.pallas_call(
        kernel,
        out_shape=jax.ShapeDtypeStruct((ROWS, SHARE), f32),
        in_specs=[spec for _, spec in operands],
        out_specs=pl.BlockSpec(memory_space=pltpu.VMEM),
        scratch_shapes=[
            vmem((KVH, 2, SLOTS, PAGE, HD), f32),
            vmem((REQS, 1, PAGES), jnp.int32),
            vmem((REQS, 1, PAGES), jnp.int32),
            vmem((2, ROWS * GROUP, 128), f32),
            vmem((ROWS, GROUP, HD), bf16),
            vmem((ROWS, 2, KVH, HD), f32),
            vmem((2, REQS, STEPS, SHARE), bf16),
            vmem((1, D), f32),
            vmem((HD, D), bf16),
            vmem((2 * D, 128), bf16),
            vmem((4 * D, 128), bf16),
            vmem((2, 2, D), bf16),
            vmem((1, 128), f32),
            vmem((2 * 128, D), bf16),
            vmem((REQS, GROUP, 2, 8, 128), f32),
            vmem((512, 128), f32),
            vmem((1024, 128), f32),
            vmem((D, 6 * 128), bf16),
            vmem((8, D), f32),
            vmem((GROUP, 64, 128), bf16),
            vmem((GROUP, 64, 128), bf16),
            vmem((GROUP, 2, 64, 128), bf16),
            vmem((2 * REQS, 256, 128), bf16),
            vmem((GROUP, ROWS, MSG), bf16),
            vmem((GROUP + 1, 2, ROWS, MSG), bf16),
            vmem((ROWS, MSG), bf16),
            vmem((ROWS, HD), bf16),
            vmem((ROWS, HD), bf16),
            vmem((GROUP, BOTH, SHARE), bf16),
            vmem((GROUP - 1, BOTH, SHARE), bf16),
            vmem((BOTH, SHARE), bf16),
            vmem((GROUP, BOTH, SHARE), bf16),
            vmem((2, GROUP, ROWS, SHARE), bf16),
            vmem((GROUP, ROWS, SHARE), bf16),
            vmem((ROWS, SHARE), f32),
            vmem((ROWS, SHARE), f32),
            pltpu.SemaphoreType.DMA((20,)),
            pltpu.SemaphoreType.DMA((11,)),
            pltpu.SemaphoreType.DMA((11,)),
            pltpu.SemaphoreType.REGULAR((LEVELS,)),
        ],
        compiler_params=pltpu.CompilerParams(
            collective_id=0, has_side_effects=True, vmem_limit_bytes=60 * 1024 * 1024
        ),
    )(*[value for value, _ in operands])
    return out.reshape(REQS, 1, STEPS, SHARE)


def solution(mesh):
    return jax.shard_map(
        body,
        mesh=mesh,
        in_specs=(
            P("req", "seq", None, None, None),
            P(None, "req", None),
            P(None, "req", None),
            P(None, "req"),
            P(None, "req", None, None, None),
            P(None, "req", None, None, None),
            P(None, "req", None, None, None, None),
            P(None, "req", None, None),
            P(),
            P("seq", None, None),
            P(None, "seq", None, None),
            P(None, "seq", None, None),
            P(None, None, "seq"),
            P("seq"),
            P("seq"),
            P(),
            P("seq", None, None),
            P(None, None, "req", "seq", None),
        ),
        out_specs=P(None, "req", None, "seq"),
        check_vma=False,
    )
```

```python
import jax
import jax.numpy as jnp
from jax import lax
from jax.experimental import pallas as pl
from jax.experimental.pallas import tpu as pltpu
from jax.sharding import PartitionSpec as P

floor_score = -1e30
norm_eps = 1e-06
MESH = pl.DeviceIdType.MESH
f32 = jnp.float32
bf16 = jnp.bfloat16

GROUP = 16
REQS = 4
STEPS = 4
ROWS = REQS * STEPS
BOTH = 2 * ROWS
LEVELS = 8
SLOTS = 48
PAGE = 16
TOKENS = SLOTS * PAGE
PAGES = 192
HD = 256
D = 2048
SHARE = 128
KVH = 2
PER_KV = 8
MSG = HD + 128
OFFSETS = [(y, x) for y in range(4) for x in range(4) if y or x]
FAR_FIRST = sorted(OFFSETS, key=lambda o: -(min(o[0], 4 - o[0]) + min(o[1], 4 - o[1])))
PLACES = (1, 0, 3, 2, 6, 5, 7, 4)
ORDER = (1, 0, 3, 2, 7, 5, 4, 6)


def dot(a, b):
    return jnp.dot(a, b, preferred_element_type=f32)


def dot_t(a, b):
    return lax.dot_general(a, b, (((1,), (1,)), ((), ())), preferred_element_type=f32)


def iota(shape, axis):
    return lax.broadcasted_iota(jnp.int32, shape, axis)


def shifted(x, by):
    return jnp.concatenate([x[-by:], x[:-by]], axis=0) if by else x


def kernel(
    kv_hbm, owner_hbm, slot_hbm, lengths, q_hbm, gates_hbm, new_hbm, tokens_hbm, gain_hbm, wo_hbm,
    wqk_hbm, wvg_hbm, wmix_hbm, decay_scale, dt_bias, dgain_hbm, wdo_hbm, state_hbm,
    out_ref,
    kv, owner, slot, q, gates, new, tokens, gain, wo, wqk, wvg, wmix, dgain, wdo, state,
    fq, fv, w_all, w_mix, s_out, s_more, s_in, held_states, m_out, m_in, draft_out, gate_out, gate_in,
    a_out, a_in, x_out, x_in, d_out, d_in, base_out, base_in,
    load_sem, send_sem, recv_sem, ready_sem,
):
    i = lax.axis_index("req")
    me = lax.axis_index("seq")
    z = i // 2
    core = lax.rem(i, 2)
    front = 2 * z + 1
    back = 2 * z
    on_front = core == 1
    on_back = core == 0

    copies = {}

    def plan(name, src, dst):
        copies[name] = pltpu.make_async_copy(src, dst, load_sem.at[len(copies)])

    own_lanes = pl.ds(pl.multiple_of(me * SHARE, SHARE), SHARE)
    plan("q", q_hbm.at[:, 0:128], q.at[0])
    plan("q_more", q_hbm.at[:, 128:256], q.at[1])
    for k in range(KVH):
        for part in range(2):
            lanes = slice(k * HD, (k + 1) * HD)
            plan(("keys", "values")[part] + str(k), kv_hbm.at[:, part, :, lanes], kv.at[k, part])
    plan("owner", owner_hbm, owner)
    plan("slot", slot_hbm, slot)
    for copy in copies.values():
        copy.start()

    def rank(level):
        place = 0
        for n, p in enumerate(PLACES):
            place = jnp.where(level == n, p, place)
        return place

    def peer(offset):
        y, x = offset
        return lax.rem(me // 4 + y, 4) * 4 + lax.rem(lax.rem(me, 4) + x, 4)

    my_rank = rank(z)
    barrier = pltpu.get_barrier_semaphore()

    def greet(where):
        pl.semaphore_signal(barrier, inc=1, device_id=where, device_id_type=MESH)

    def each_state_source(use):
        for d in range(GROUP):
            use((2 * (me // 2), lax.rem(me + d, GROUP)))

    @pl.when(on_back)
    def _():
        greet((front, me))

    @pl.when(on_front)
    def _():
        for offset in FAR_FIRST:
            greet((back, peer(offset)))
            greet((front, peer(offset)))
        greet((back, me))

    early_receiver = on_front & (my_rank < rank(me // 2))
    own_receiver = on_front & (z == me // 2)
    late_receiver = on_front & (my_rank > rank(me // 2))

    @pl.when(early_receiver)
    def _():
        for d in range(GROUP):
            greet((me, lax.rem(me + d, GROUP)))

    @pl.when(own_receiver)
    def _():
        each_state_source(greet)

    for d in range(1, LEVELS):
        level = lax.rem(z + d, LEVELS)

        @pl.when(on_back & (rank(level) > my_rank))
        def _():
            for c in range(2):
                greet((2 * level + 1, 2 * z + c))

    copies["owner"].wait()
    copies["slot"].wait()
    page_at = iota((SLOTS, PAGES), 1)
    slot_at = iota((SLOTS, PAGES), 0)
    row_request = lax.rem(iota((SLOTS, 128), 1) // STEPS, REQS)
    counts = jnp.zeros((SLOTS, 128), f32)
    for r in range(REQS):
        live = jnp.clip(lengths[r] - page_at * PAGE, 0, PAGE)
        held = (owner[r] == me) & (slot[r] == slot_at)
        count = jnp.sum(jnp.where(held, live, 0).astype(f32), axis=1, keepdims=True)
        counts = jnp.where(row_request == r, count, counts)
    in_page = iota((SLOTS, PAGE, 128), 1).astype(f32)
    live_mask = (in_page < counts[:, None, :]).reshape(TOKENS, 128)

    def head_queries(h):
        halves = [q[half, pl.ds(h, ROWS, stride=GROUP), :] for half in range(2)]
        return jnp.concatenate(halves, axis=1) * (HD ** -0.5)

    def part_stats(top, total):
        lane = iota((top.shape[0], 128), 1)
        total_hi = total.astype(bf16).astype(f32)
        stats = jnp.where(lane == 0, top, jnp.where(lane == 1, total_hi, total - total_hi))
        return stats.astype(bf16)

    plan("state", state_hbm, state)
    plan("gates", gates_hbm, gates)
    plan("new", new_hbm, new)
    plan("wqk", wqk_hbm, wqk)
    plan("wvg", wvg_hbm, wvg)
    plan("wmix", wmix_hbm, wmix)
    plan("wo", wo_hbm, wo)
    plan("tokens", tokens_hbm.at[:, 0, :, own_lanes], tokens.at[1])
    plan("gain", gain_hbm, gain)
    plan("dgain", dgain_hbm, dgain)
    plan("wdo", wdo_hbm, wdo)

    copies["q"].wait()
    copies["q_more"].wait()
    for k in range(KVH):
        queries = jnp.concatenate([head_queries(k * PER_KV + h) for h in range(PER_KV)], axis=0)
        q_hi = queries.astype(bf16)
        q_lo = (queries - q_hi.astype(f32)).astype(bf16)
        copies["keys" + str(k)].wait()
        keys = kv[k, 0].reshape(TOKENS, HD)
        k_hi = keys.astype(bf16)
        k_lo = (keys - k_hi.astype(f32)).astype(bf16)
        by_hi = dot_t(k_hi, jnp.concatenate([q_hi, q_lo], axis=0))
        scores = by_hi[:, :128] + (by_hi[:, 128:] + dot_t(k_lo, q_hi))
        scores = jnp.where(live_mask, scores, floor_score)
        top = jnp.max(scores, axis=0, keepdims=True).astype(bf16).astype(f32)
        weights = jnp.where(live_mask, jnp.exp(scores - top), 0.0).astype(bf16)
        total = jnp.sum(weights.astype(f32), axis=0, keepdims=True)
        copies["values" + str(k)].wait()
        values = kv[k, 1].reshape(TOKENS, HD).astype(bf16)
        own = pl.ds(k * PER_KV, PER_KV)
        acc = lax.dot_general(weights, values, (((0,), (0,)), ((), ())), preferred_element_type=f32)
        m_out[own, :, 0:HD] = acc.astype(bf16).reshape(PER_KV, ROWS, HD)
        total_hi = total.astype(bf16).astype(f32)
        sides = jnp.concatenate([top, total_hi, total - total_hi, jnp.zeros((125, 128), f32)], axis=0)
        m_out[own, :, HD:MSG] = sides.T.astype(bf16).reshape(PER_KV, ROWS, 128)

    for name in ("state", "gates", "new"):
        copies[name].start()

    @pl.when(on_front)
    def _():
        for name in ("wqk", "wvg", "wmix", "wo", "tokens", "gain", "dgain", "wdo"):
            copies[name].start()

    pl.semaphore_wait(
        barrier,
        jnp.where(
            on_front,
            GROUP + my_rank + GROUP * late_receiver.astype(jnp.int32),
            GROUP + my_rank + 2,
        ),
    )

    def send(src, dst, phase, where, sent_at=None):
        pltpu.make_async_remote_copy(
            src_ref=src,
            dst_ref=dst,
            send_sem=send_sem.at[phase if sent_at is None else sent_at],
            recv_sem=recv_sem.at[phase],
            device_id=where,
            device_id_type=MESH,
        ).start()

    def arrived(ref, phase):
        pltpu.make_async_copy(ref, ref, recv_sem.at[phase]).wait()

    def sent(ref, phase):
        pltpu.make_async_copy(ref, ref, send_sem.at[phase]).wait()

    for n, offset in enumerate(FAR_FIRST):
        other = peer(offset)
        send(m_out.at[other], m_in.at[n, core], 0, (front, other))

    @pl.when(on_back)
    def _():
        send(m_out.at[me], m_in.at[GROUP - 1, 0], 0, (front, me))
        send(tokens_hbm.at[:, 0, :, own_lanes], tokens.at[0], 9, (front, me))

    @pl.when(late_receiver)
    def _():
        each_state_source(
            lambda source: pl.semaphore_signal(
                ready_sem.at[z], inc=1, device_id=source, device_id_type=MESH
            )
        )

    copies["new"].wait()
    copies["gates"].wait()
    own_q = head_queries(me)
    low_kv = me < PER_KV

    def draft(component):
        both = new[:, component].astype(f32)
        return jnp.where(low_kv, both[:, 0], both[:, 1])

    draft_scores = lax.dot_general(
        own_q, draft(0), (((1,), (1,)), ((), ())),
        preferred_element_type=f32, precision=lax.Precision.HIGHEST,
    )
    row, col = iota((ROWS, ROWS), 0), iota((ROWS, ROWS), 1)
    causal = (row // STEPS == col // STEPS) & (col <= row)
    draft_scores = jnp.where(causal, draft_scores, floor_score)
    draft_top = jnp.max(draft_scores, axis=1, keepdims=True).astype(bf16).astype(f32)
    draft_weights = jnp.where(causal, jnp.exp(draft_scores - draft_top), 0.0)
    draft_acc = lax.dot_general(
        draft_weights, draft(1), (((1,), (0,)), ((), ())),
        preferred_element_type=f32, precision=lax.Precision.HIGHEST,
    )
    draft_out[:, 0:HD] = draft_acc.astype(bf16)
    draft_out[:, HD:MSG] = part_stats(draft_top, jnp.sum(draft_weights, axis=1, keepdims=True))
    own_gate = jnp.sum(
        jnp.where(iota((ROWS, GROUP, HD), 1) == me, gates[...].astype(f32), 0.0), axis=1
    )
    gate_out[...] = own_gate.astype(bf16)

    @pl.when(on_back)
    def _():
        send(draft_out, m_in.at[GROUP, 0], 0, (front, me))
        send(gate_out, gate_in, 8, (front, me))

    copies["state"].wait()
    for g in range(GROUP):
        s_out[g] = state[:, g].reshape(REQS * 2 * 8, 128).astype(bf16)

    def send_states(src, c, phase_sent, chosen):
        for d in range(LEVELS):
            level = lax.rem(z + me + d, LEVELS)

            @pl.when(chosen(rank(level)))
            def _():
                send(src.at[pl.ds(2 * level, 2)], s_in.at[me], 1, (2 * level + 1, 2 * z + c), phase_sent)

    @pl.when(on_back)
    def _():
        send_states(s_out, 0, 1, lambda place: place <= my_rank)
        arrived(s_more, 5)
        send_states(s_more, 1, 6, lambda place: place == my_rank)

        for r, level in enumerate(ORDER):
            @pl.when(my_rank < r)
            def _():
                pl.semaphore_wait(ready_sem.at[level], 2)
                for c in range(2):
                    send(
                        (s_out, s_more)[c].at[pl.ds(2 * level, 2)], s_in.at[me], 1, (2 * level + 1, 2 * z + c), (1, 6)[c]
                    )

        sent(s_out, 1)
        for r in range(LEVELS):

            @pl.when(my_rank == r)
            def _():
                sent(s_more.at[pl.ds(0, 2 * (LEVELS - r))], 6)

    @pl.when(on_front)
    def _():
        send_states(s_out, 1, 1, lambda place: place < my_rank)
        send(s_out, s_more, 5, (back, me))

    @pl.when(on_back)
    def _():
        sent(m_in.at[:, 0], 0)
        sent(tokens.at[0], 9)
        sent(gate_in, 8)
        arrived(base_in, 10)
        arrived(d_in, 4)
        result = base_in[...]
        for n in range(GROUP):
            result = result + d_in[n].astype(f32)
        out_ref[...] = result

    @pl.when(on_front)
    def _():
        m_in[GROUP - 1, 1] = m_out[me]
        m_in[GROUP, 1] = draft_out[...]

        copies["wqk"].wait()
        copies["wvg"].wait()
        chunk = 256

        def arrange(c, carry):
            rows = pl.ds(pl.multiple_of(c * chunk, chunk), chunk)
            fq[...] = wqk[pl.ds(pl.multiple_of(c * (2 * chunk), 2 * chunk), 2 * chunk), :].astype(f32)
            fv[...] = wvg[pl.ds(pl.multiple_of(c * (4 * chunk), 4 * chunk), 4 * chunk), :].astype(f32)
            for n in range(2):
                w_all[rows, n * 128 : (n + 1) * 128] = fq[pl.ds(n, chunk, stride=2), :].astype(bf16)
            for n in range(4):
                w_all[rows, (n + 2) * 128 : (n + 3) * 128] = fv[pl.ds(n, chunk, stride=4), :].astype(bf16)
            return carry

        lax.fori_loop(0, D // chunk, arrange, 0)
        copies["wmix"].wait()
        for n in range(2):
            w_mix[2 * n : 2 * n + 2, :] = wmix[n].astype(f32)
        for name in ("wo", "tokens", "gain", "dgain", "wdo"):
            copies[name].wait()
        arrived(gate_in, 8)
        arrived(tokens.at[0], 9)
        gate = jax.nn.sigmoid(jnp.concatenate([gate_in[...], gate_out[...]], axis=0).astype(f32))

        arrived(m_in.at[pl.ds(0, GROUP)], 0)
        parts = [m_in[n].reshape(BOTH, MSG) for n in range(GROUP + 1)]
        ceiling = parts[0][:, HD : HD + 1].astype(f32)
        for part in parts[1:]:
            ceiling = jnp.maximum(ceiling, part[:, HD : HD + 1].astype(f32))
        total = jnp.zeros((BOTH, 1), f32)
        acc = jnp.zeros((BOTH, HD), f32)
        for part in parts:
            stats = part[:, HD:MSG].astype(f32)
            factor = jnp.exp(stats[:, 0:1] - ceiling)
            total = total + factor * (stats[:, 1:2] + stats[:, 2:3])
            acc = acc + factor * part[:, 0:HD].astype(f32)
        gated = (acc / total * gate).astype(bf16)

        total = dot(gated, wo[...])
        for e in range(GROUP):
            a_out[e] = total[:, e * SHARE : (e + 1) * SHARE].astype(bf16)
        for n, offset in enumerate(FAR_FIRST):
            other = peer(offset)
            send(a_out.at[other], a_in.at[n], 2, (front, other))
        stream = tokens[...].astype(f32).reshape(BOTH, SHARE) + a_out[me].astype(f32)
        arrived(a_in, 2)
        for n in range(GROUP - 1):
            stream = stream + a_in[n].astype(f32)

        own_x = (stream * gain[:, own_lanes]).astype(bf16)
        x_out[...] = own_x
        x_in[me] = own_x
        for offset in FAR_FIRST:
            send(x_out, x_in.at[me], 3, (front, peer(offset)))
        base_out[...] = stream[0:ROWS]
        send(base_out, base_in, 10, (back, me))

        arrived(s_in, 1)
        for g in range(2):
            for r in range(REQS):
                rows = s_in[:, g, r * 16 : (r + 1) * 16].astype(f32).reshape(GROUP, 2, 8, 128)
                blocks = [rows[j, h] for h in range(2) for j in range(GROUP)]
                held_states[g * REQS + r] = jnp.concatenate(blocks, axis=0).astype(bf16)

        inverse = 1.0 / gain[...]
        arrived(x_in.at[pl.ds(0, GROUP - 1)], 3)
        y = jnp.concatenate([x_in[e] for e in range(GROUP)], axis=1)
        proj = dot(y, w_all[...])
        y = y.astype(f32)
        mixes = [jnp.sum(y * w_mix[c : c + 1], axis=1, keepdims=True) for c in range(4)]
        x = y * inverse
        squares = jnp.sum(x * x, axis=1, keepdims=True)
        scale = lax.rsqrt(squares * (1.0 / D) + norm_eps)
        proj = proj * scale
        mixes = [mix * scale for mix in mixes]

        def unit(x):
            return x * lax.rsqrt(jnp.sum(x * x, axis=1, keepdims=True) + norm_eps)

        dq = unit(proj[:, 0:128])
        dk = unit(proj[:, 128:256])
        value = jnp.concatenate([proj[:, 256:384], proj[:, 512:640]], axis=1)
        zgate = jnp.concatenate([proj[:, 384:512], proj[:, 640:768]], axis=1)
        wide = (BOTH, 2 * 128)
        high = iota(wide, 1) >= 128
        beta = jnp.where(high, jax.nn.sigmoid(mixes[1]), jax.nn.sigmoid(mixes[0]))

        def decay_of(h):
            t = mixes[2 + h] + dt_bias[h]
            soft = jnp.maximum(t, 0.0) + jnp.log(1.0 + jnp.exp(-jnp.abs(t)))
            return jnp.exp(-decay_scale[h] * soft)

        decay = jnp.where(high, decay_of(1), decay_of(0))

        both = jnp.concatenate([dk, dq], axis=0).astype(bf16)
        row_of = lax.rem(iota((2 * BOTH, 2 * 128), 0) // STEPS, 2 * REQS)
        prior = jnp.zeros((2 * BOTH, 2 * 128), f32)
        for r in range(2 * REQS):
            prior = jnp.where(row_of == r, dot_t(both, held_states[r]), prior)
        prior_k, prior_q = prior[:BOTH], prior[BOTH:]
        step = lax.rem(iota(wide, 0), STEPS)
        ratio = [jnp.ones(wide, f32), decay]
        for o in range(1, STEPS):
            ratio.append(decay * shifted(ratio[o], 1))
        whole = jnp.where(
            step == 0, ratio[1], jnp.where(step == 1, ratio[2], jnp.where(step == 2, ratio[3], ratio[4]))
        )
        key_back = [shifted(dk, o) for o in range(STEPS)]
        beta_prior = beta * (value - whole * prior_k)
        coupling = [
            jnp.where(step >= o, beta * ratio[o] * jnp.sum(dk * key_back[o], axis=1, keepdims=True), 0.0)
            for o in range(1, STEPS)
        ]
        update = beta_prior
        for _ in range(STEPS - 1):
            following = beta_prior
            for o in range(1, STEPS):
                following = following - coupling[o - 1] * shifted(update, o)
            update = following
        readout = whole * prior_q
        for o in range(STEPS):
            reach = jnp.sum(dq * key_back[o], axis=1, keepdims=True)
            readout = readout + jnp.where(step >= o, ratio[o] * reach, 0.0) * shifted(update, o)
        readout = readout * (128 ** -0.5)

        def normal(x):
            return x * lax.rsqrt(jnp.mean(x * x, axis=1, keepdims=True) + norm_eps) * dgain[...]

        normalized = jnp.concatenate([normal(readout[:, :128]), normal(readout[:, 128:])], axis=1)
        normalized = (normalized * zgate * jax.nn.sigmoid(zgate)).astype(bf16)

        total = dot(normalized, wdo[...])
        for e in range(GROUP):
            d_out[:, e] = total[:, e * SHARE : (e + 1) * SHARE].astype(bf16).reshape(2, ROWS, SHARE)
        for n, offset in enumerate(FAR_FIRST):
            other = peer(offset)
            send(d_out.at[1, other], d_in.at[n], 4, (front, other))
        for n, offset in enumerate(FAR_FIRST):
            other = peer(offset)
            send(d_out.at[0, other], d_in.at[n], 4, (back, other))
        send(d_out.at[0, me], d_in.at[GROUP - 1], 4, (back, me))
        result = stream[ROWS:BOTH] + d_out[1, me].astype(f32)
        sent(m_in.at[pl.ds(0, GROUP - 1), 0], 0)
        sent(s_more, 5)
        for r in range(1, LEVELS):

            @pl.when(my_rank == r)
            def _():
                sent(s_out.at[pl.ds(0, 2 * r)], 1)

        sent(a_in, 2)
        sent(x_in.at[pl.ds(0, GROUP - 1)], 3)
        sent(base_out, 10)
        arrived(d_in.at[pl.ds(0, GROUP - 1)], 4)
        for n in range(GROUP - 1):
            result = result + d_in[n].astype(f32)
        out_ref[...] = result
        sent(d_out.at[0], 4)
        sent(d_out.at[1, pl.ds(0, GROUP - 1)], 4)


def body(
    kv_pool, page_owner, page_slot, lengths, queries, gates, new_kv, tokens, attn_gain, out_heads,
    w_query_key, w_value_gate, w_beta_decay, decay_scale, dt_bias, delta_gain, w_delta_out, prior_state,
):
    hbm = pl.BlockSpec(memory_space=pl.ANY)
    smem = pl.BlockSpec(memory_space=pltpu.SMEM)
    vmem = pltpu.VMEM
    operands = (
        (kv_pool.reshape(SLOTS, 2, PAGE, KVH * HD), hbm),
        (page_owner, hbm),
        (page_slot, hbm),
        (lengths.reshape(REQS), smem),
        (queries.reshape(ROWS * GROUP, HD), hbm),
        (gates.reshape(ROWS, GROUP, HD), hbm),
        (new_kv.reshape(ROWS, 2, KVH, HD), hbm),
        (tokens, hbm),
        (attn_gain.reshape(1, D), hbm),
        (out_heads.reshape(HD, D), hbm),
        (w_query_key.reshape(2 * D, 128), hbm),
        (w_value_gate.reshape(4 * D, 128), hbm),
        (w_beta_decay.transpose(1, 2, 0), hbm),
        (decay_scale, smem),
        (dt_bias, smem),
        (delta_gain.reshape(1, 128), hbm),
        (w_delta_out.reshape(2 * 128, D), hbm),
        (prior_state, hbm),
    )
    out = pl.pallas_call(
        kernel,
        out_shape=jax.ShapeDtypeStruct((ROWS, SHARE), f32),
        in_specs=[spec for _, spec in operands],
        out_specs=pl.BlockSpec(memory_space=pltpu.VMEM),
        scratch_shapes=[
            vmem((KVH, 2, SLOTS, PAGE, HD), f32),
            vmem((REQS, 1, PAGES), jnp.int32),
            vmem((REQS, 1, PAGES), jnp.int32),
            vmem((2, ROWS * GROUP, 128), f32),
            vmem((ROWS, GROUP, HD), bf16),
            vmem((ROWS, 2, KVH, HD), f32),
            vmem((2, REQS, STEPS, SHARE), bf16),
            vmem((1, D), f32),
            vmem((HD, D), bf16),
            vmem((2 * D, 128), bf16),
            vmem((4 * D, 128), bf16),
            vmem((2, 2, D), bf16),
            vmem((1, 128), f32),
            vmem((2 * 128, D), bf16),
            vmem((REQS, GROUP, 2, 8, 128), f32),
            vmem((512, 128), f32),
            vmem((1024, 128), f32),
            vmem((D, 6 * 128), bf16),
            vmem((8, D), f32),
            vmem((GROUP, 64, 128), bf16),
            vmem((GROUP, 64, 128), bf16),
            vmem((GROUP, 2, 64, 128), bf16),
            vmem((2 * REQS, 256, 128), bf16),
            vmem((GROUP, ROWS, MSG), bf16),
            vmem((GROUP + 1, 2, ROWS, MSG), bf16),
            vmem((ROWS, MSG), bf16),
            vmem((ROWS, HD), bf16),
            vmem((ROWS, HD), bf16),
            vmem((GROUP, BOTH, SHARE), bf16),
            vmem((GROUP - 1, BOTH, SHARE), bf16),
            vmem((BOTH, SHARE), bf16),
            vmem((GROUP, BOTH, SHARE), bf16),
            vmem((2, GROUP, ROWS, SHARE), bf16),
            vmem((GROUP, ROWS, SHARE), bf16),
            vmem((ROWS, SHARE), f32),
            vmem((ROWS, SHARE), f32),
            pltpu.SemaphoreType.DMA((20,)),
            pltpu.SemaphoreType.DMA((11,)),
            pltpu.SemaphoreType.DMA((11,)),
            pltpu.SemaphoreType.REGULAR((LEVELS,)),
        ],
        compiler_params=pltpu.CompilerParams(
            collective_id=0, has_side_effects=True, vmem_limit_bytes=60 * 1024 * 1024
        ),
    )(*[value for value, _ in operands])
    return out.reshape(REQS, 1, STEPS, SHARE)


def solution(mesh):
    return jax.shard_map(
        body,
        mesh=mesh,
        in_specs=(
            P("req", "seq", None, None, None),
            P(None, "req", None),
            P(None, "req", None),
            P(None, "req"),
            P(None, "req", None, None, None),
            P(None, "req", None, None, None),
            P(None, "req", None, None, None, None),
            P(None, "req", None, None),
            P(),
            P("seq", None, None),
            P(None, "seq", None, None),
            P(None, "seq", None, None),
            P(None, None, "seq"),
            P("seq"),
            P("seq"),
            P(),
            P("seq", None, None),
            P(None, None, "req", "seq", None),
        ),
        out_specs=P(None, "req", None, "seq"),
        check_vma=False,
    )
```

```python
import jax
import jax.numpy as jnp
from jax import lax
from jax.experimental import pallas as pl
from jax.experimental.pallas import tpu as pltpu
from jax.sharding import PartitionSpec as P

floor_score = -1e30
norm_eps = 1e-06
MESH = pl.DeviceIdType.MESH
f32 = jnp.float32
bf16 = jnp.bfloat16

GROUP = 16
REQS = 4
STEPS = 4
ROWS = REQS * STEPS
BOTH = 2 * ROWS
LEVELS = 8
SLOTS = 48
PAGE = 16
TOKENS = SLOTS * PAGE
PAGES = 192
HD = 256
D = 2048
SHARE = 128
KVH = 2
PER_KV = 8
MSG = HD + 128
OFFSETS = [(y, x) for y in range(4) for x in range(4) if y or x]
FAR_FIRST = sorted(OFFSETS, key=lambda o: -(min(o[0], 4 - o[0]) + min(o[1], 4 - o[1])))
PLACES = (1, 0, 3, 2, 6, 5, 7, 4)
ORDER = (1, 0, 3, 2, 7, 5, 4, 6)


def dot(a, b):
    return jnp.dot(a, b, preferred_element_type=f32)


def dot_t(a, b):
    return lax.dot_general(a, b, (((1,), (1,)), ((), ())), preferred_element_type=f32)


def iota(shape, axis):
    return lax.broadcasted_iota(jnp.int32, shape, axis)


def shifted(x, by):
    return jnp.concatenate([x[-by:], x[:-by]], axis=0) if by else x


def kernel(
    kv_hbm, owner_hbm, slot_hbm, lengths, q_hbm, gates_hbm, new_hbm, tokens_hbm, gain_hbm, wo_hbm,
    wqk_hbm, wvg_hbm, wmix_hbm, decay_scale, dt_bias, dgain_hbm, wdo_hbm, state_hbm,
    out_ref,
    kv, owner, slot, q, gates, new, tokens, gain, wo, wqk, wvg, wmix, dgain, wdo, state,
    fq, fv, w_all, w_mix, s_out, s_more, s_in, held_states, m_out, m_in, draft_out, gate_out, gate_in,
    a_out, a_in, x_out, x_in, d_out, d_in, base_out, base_in,
    load_sem, send_sem, recv_sem, ready_sem,
):
    i = lax.axis_index("req")
    me = lax.axis_index("seq")
    z = i // 2
    core = lax.rem(i, 2)
    front = 2 * z + 1
    back = 2 * z
    on_front = core == 1
    on_back = core == 0

    copies = {}

    def plan(name, src, dst):
        copies[name] = pltpu.make_async_copy(src, dst, load_sem.at[len(copies)])

    own_lanes = pl.ds(pl.multiple_of(me * SHARE, SHARE), SHARE)
    plan("q", q_hbm.at[:, 0:128], q.at[0])
    plan("q_more", q_hbm.at[:, 128:256], q.at[1])
    for k in range(KVH):
        for part in range(2):
            lanes = slice(k * HD, (k + 1) * HD)
            plan(("keys", "values")[part] + str(k), kv_hbm.at[:, part, :, lanes], kv.at[k, part])
    plan("owner", owner_hbm, owner)
    plan("slot", slot_hbm, slot)
    for copy in copies.values():
        copy.start()

    def rank(level):
        place = 0
        for n, p in enumerate(PLACES):
            place = jnp.where(level == n, p, place)
        return place

    def peer(offset):
        y, x = offset
        return lax.rem(me // 4 + y, 4) * 4 + lax.rem(lax.rem(me, 4) + x, 4)

    my_rank = rank(z)
    barrier = pltpu.get_barrier_semaphore()

    def greet(where):
        pl.semaphore_signal(barrier, inc=1, device_id=where, device_id_type=MESH)

    def each_state_source(use):
        for d in range(GROUP):
            use((2 * (me // 2), lax.rem(me + d, GROUP)))

    @pl.when(on_back)
    def _():
        greet((front, me))

    @pl.when(on_front)
    def _():
        for offset in FAR_FIRST:
            greet((back, peer(offset)))
            greet((front, peer(offset)))
        greet((back, me))

    early_receiver = on_front & (my_rank < rank(me // 2))
    own_receiver = on_front & (z == me // 2)
    late_receiver = on_front & (my_rank > rank(me // 2))

    @pl.when(early_receiver)
    def _():
        for d in range(GROUP):
            greet((me, lax.rem(me + d, GROUP)))

    @pl.when(own_receiver)
    def _():
        each_state_source(greet)

    for d in range(1, LEVELS):
        level = lax.rem(z + d, LEVELS)

        @pl.when(on_back & (rank(level) > my_rank))
        def _():
            for c in range(2):
                greet((2 * level + 1, 2 * z + c))

    copies["owner"].wait()
    copies["slot"].wait()
    page_at = iota((SLOTS, PAGES), 1)
    slot_at = iota((SLOTS, PAGES), 0)
    row_request = lax.rem(iota((SLOTS, 128), 1) // STEPS, REQS)
    counts = jnp.zeros((SLOTS, 128), f32)
    for r in range(REQS):
        live = jnp.clip(lengths[r] - page_at * PAGE, 0, PAGE)
        held = (owner[r] == me) & (slot[r] == slot_at)
        count = jnp.sum(jnp.where(held, live, 0).astype(f32), axis=1, keepdims=True)
        counts = jnp.where(row_request == r, count, counts)
    in_page = iota((SLOTS, PAGE, 128), 1).astype(f32)
    live_mask = (in_page < counts[:, None, :]).reshape(TOKENS, 128)

    def head_queries(h):
        halves = [q[half, pl.ds(h, ROWS, stride=GROUP), :] for half in range(2)]
        return jnp.concatenate(halves, axis=1) * (HD ** -0.5)

    def part_stats(top, total):
        lane = iota((top.shape[0], 128), 1)
        total_hi = total.astype(bf16).astype(f32)
        stats = jnp.where(lane == 0, top, jnp.where(lane == 1, total_hi, total - total_hi))
        return stats.astype(bf16)

    plan("state", state_hbm, state)
    plan("gates", gates_hbm, gates)
    plan("new", new_hbm, new)
    plan("wqk", wqk_hbm, wqk)
    plan("wvg", wvg_hbm, wvg)
    plan("wmix", wmix_hbm, wmix)
    plan("wo", wo_hbm, wo)
    plan("tokens", tokens_hbm.at[:, 0, :, own_lanes], tokens.at[1])
    plan("gain", gain_hbm, gain)
    plan("dgain", dgain_hbm, dgain)
    plan("wdo", wdo_hbm, wdo)

    copies["q"].wait()
    copies["q_more"].wait()
    for k in range(KVH):
        queries = jnp.concatenate([head_queries(k * PER_KV + h) for h in range(PER_KV)], axis=0)
        q_hi = queries.astype(bf16)
        q_lo = (queries - q_hi.astype(f32)).astype(bf16)
        copies["keys" + str(k)].wait()
        keys = kv[k, 0].reshape(TOKENS, HD)
        k_hi = keys.astype(bf16)
        k_lo = (keys - k_hi.astype(f32)).astype(bf16)
        by_hi = dot_t(k_hi, jnp.concatenate([q_hi, q_lo], axis=0))
        scores = by_hi[:, :128] + (by_hi[:, 128:] + dot_t(k_lo, q_hi))
        scores = jnp.where(live_mask, scores, floor_score)
        top = jnp.max(scores, axis=0, keepdims=True).astype(bf16).astype(f32)
        weights = jnp.where(live_mask, jnp.exp(scores - top), 0.0).astype(bf16)
        total = jnp.sum(weights.astype(f32), axis=0, keepdims=True)
        copies["values" + str(k)].wait()
        values = kv[k, 1].reshape(TOKENS, HD).astype(bf16)
        own = pl.ds(k * PER_KV, PER_KV)
        acc = lax.dot_general(weights, values, (((0,), (0,)), ((), ())), preferred_element_type=f32)
        m_out[own, :, 0:HD] = acc.astype(bf16).reshape(PER_KV, ROWS, HD)
        total_hi = total.astype(bf16).astype(f32)
        sides = jnp.concatenate([top, total_hi, total - total_hi, jnp.zeros((125, 128), f32)], axis=0)
        m_out[own, :, HD:MSG] = sides.T.astype(bf16).reshape(PER_KV, ROWS, 128)

    for name in ("state", "gates", "new"):
        copies[name].start()

    @pl.when(on_front)
    def _():
        for name in ("wqk", "wvg", "wmix", "wo", "tokens", "gain", "dgain", "wdo"):
            copies[name].start()

    pl.semaphore_wait(
        barrier,
        jnp.where(
            on_front,
            GROUP + my_rank + GROUP * late_receiver.astype(jnp.int32),
            GROUP + my_rank + 2,
        ),
    )

    def send(src, dst, phase, where, sent_at=None):
        pltpu.make_async_remote_copy(
            src_ref=src,
            dst_ref=dst,
            send_sem=send_sem.at[phase if sent_at is None else sent_at],
            recv_sem=recv_sem.at[phase],
            device_id=where,
            device_id_type=MESH,
        ).start()

    def arrived(ref, phase):
        pltpu.make_async_copy(ref, ref, recv_sem.at[phase]).wait()

    def sent(ref, phase):
        pltpu.make_async_copy(ref, ref, send_sem.at[phase]).wait()

    for n, offset in enumerate(FAR_FIRST):
        other = peer(offset)
        send(m_out.at[other], m_in.at[n, core], 0, (front, other))

    @pl.when(on_back)
    def _():
        send(m_out.at[me], m_in.at[GROUP - 1, 0], 0, (front, me))
        send(tokens_hbm.at[:, 0, :, own_lanes], tokens.at[0], 9, (front, me))

    @pl.when(late_receiver)
    def _():
        each_state_source(
            lambda source: pl.semaphore_signal(
                ready_sem.at[z], inc=1, device_id=source, device_id_type=MESH
            )
        )

    copies["new"].wait()
    copies["gates"].wait()
    own_q = head_queries(me)
    low_kv = me < PER_KV

    def draft(component):
        both = new[:, component].astype(f32)
        return jnp.where(low_kv, both[:, 0], both[:, 1])

    draft_scores = lax.dot_general(
        own_q, draft(0), (((1,), (1,)), ((), ())),
        preferred_element_type=f32, precision=lax.Precision.HIGHEST,
    )
    row, col = iota((ROWS, ROWS), 0), iota((ROWS, ROWS), 1)
    causal = (row // STEPS == col // STEPS) & (col <= row)
    draft_scores = jnp.where(causal, draft_scores, floor_score)
    draft_top = jnp.max(draft_scores, axis=1, keepdims=True).astype(bf16).astype(f32)
    draft_weights = jnp.where(causal, jnp.exp(draft_scores - draft_top), 0.0)
    draft_acc = lax.dot_general(
        draft_weights, draft(1), (((1,), (0,)), ((), ())),
        preferred_element_type=f32, precision=lax.Precision.HIGHEST,
    )
    draft_out[:, 0:HD] = draft_acc.astype(bf16)
    draft_out[:, HD:MSG] = part_stats(draft_top, jnp.sum(draft_weights, axis=1, keepdims=True))
    own_gate = jnp.sum(
        jnp.where(iota((ROWS, GROUP, HD), 1) == me, gates[...].astype(f32), 0.0), axis=1
    )
    gate_out[...] = own_gate.astype(bf16)

    @pl.when(on_back)
    def _():
        send(draft_out, m_in.at[GROUP, 0], 0, (front, me))
        send(gate_out, gate_in, 8, (front, me))

    copies["state"].wait()
    for g in range(GROUP):
        s_out[g] = state[:, g].reshape(REQS * 2 * 8, 128).astype(bf16)

    def send_states(src, c, phase_sent, chosen):
        for d in range(LEVELS):
            level = lax.rem(z + me + d, LEVELS)

            @pl.when(chosen(rank(level)))
            def _():
                send(src.at[pl.ds(2 * level, 2)], s_in.at[me], 1, (2 * level + 1, 2 * z + c), phase_sent)

    @pl.when(on_back)
    def _():
        send_states(s_out, 0, 1, lambda place: place <= my_rank)
        arrived(s_more, 5)
        send_states(s_more, 1, 6, lambda place: place == my_rank)

        for r, level in enumerate(ORDER):
            @pl.when(my_rank < r)
            def _():
                pl.semaphore_wait(ready_sem.at[level], 2)
                for c in range(2):
                    send(
                        (s_out, s_more)[c].at[pl.ds(2 * level, 2)], s_in.at[me], 1, (2 * level + 1, 2 * z + c), (1, 6)[c]
                    )

        sent(s_out, 1)
        for r in range(LEVELS):

            @pl.when(my_rank == r)
            def _():
                sent(s_more.at[pl.ds(0, 2 * (LEVELS - r))], 6)

    @pl.when(on_front)
    def _():
        send_states(s_out, 1, 1, lambda place: place < my_rank)
        send(s_out, s_more, 5, (back, me))

    @pl.when(on_back)
    def _():
        sent(m_in.at[:, 0], 0)
        sent(tokens.at[0], 9)
        sent(gate_in, 8)
        arrived(base_in, 10)
        arrived(d_in, 4)
        result = base_in[...]
        for n in range(GROUP):
            result = result + d_in[n].astype(f32)
        out_ref[...] = result

    @pl.when(on_front)
    def _():
        m_in[GROUP - 1, 1] = m_out[me]
        m_in[GROUP, 1] = draft_out[...]

        copies["wqk"].wait()
        copies["wvg"].wait()
        chunk = 256

        def arrange(c, carry):
            rows = pl.ds(pl.multiple_of(c * chunk, chunk), chunk)
            fq[...] = wqk[pl.ds(pl.multiple_of(c * (2 * chunk), 2 * chunk), 2 * chunk), :].astype(f32)
            fv[...] = wvg[pl.ds(pl.multiple_of(c * (4 * chunk), 4 * chunk), 4 * chunk), :].astype(f32)
            for n in range(2):
                w_all[rows, n * 128 : (n + 1) * 128] = fq[pl.ds(n, chunk, stride=2), :].astype(bf16)
            for n in range(4):
                w_all[rows, (n + 2) * 128 : (n + 3) * 128] = fv[pl.ds(n, chunk, stride=4), :].astype(bf16)
            return carry

        lax.fori_loop(0, D // chunk, arrange, 0)
        copies["wmix"].wait()
        for n in range(2):
            w_mix[2 * n : 2 * n + 2, :] = wmix[n].astype(f32)
        for name in ("wo", "tokens", "gain", "dgain", "wdo"):
            copies[name].wait()
        arrived(gate_in, 8)
        arrived(tokens.at[0], 9)
        gate = jax.nn.sigmoid(jnp.concatenate([gate_in[...], gate_out[...]], axis=0).astype(f32))

        arrived(m_in.at[pl.ds(0, GROUP)], 0)
        parts = [m_in[n].reshape(BOTH, MSG) for n in range(GROUP + 1)]
        ceiling = parts[0][:, HD : HD + 1].astype(f32)
        for part in parts[1:]:
            ceiling = jnp.maximum(ceiling, part[:, HD : HD + 1].astype(f32))
        total = jnp.zeros((BOTH, 1), f32)
        acc = jnp.zeros((BOTH, HD), f32)
        for part in parts:
            stats = part[:, HD:MSG].astype(f32)
            factor = jnp.exp(stats[:, 0:1] - ceiling)
            total = total + factor * (stats[:, 1:2] + stats[:, 2:3])
            acc = acc + factor * part[:, 0:HD].astype(f32)
        gated = (acc / total * gate).astype(bf16)

        total = dot(gated, wo[...])
        for e in range(GROUP):
            a_out[e] = total[:, e * SHARE : (e + 1) * SHARE].astype(bf16)
        for n, offset in enumerate(FAR_FIRST):
            other = peer(offset)
            send(a_out.at[other], a_in.at[n], 2, (front, other))
        stream = tokens[...].astype(f32).reshape(BOTH, SHARE) + a_out[me].astype(f32)
        arrived(a_in, 2)
        for n in range(GROUP - 1):
            stream = stream + a_in[n].astype(f32)

        own_x = (stream * gain[:, own_lanes]).astype(bf16)
        x_out[...] = own_x
        x_in[me] = own_x
        for offset in FAR_FIRST:
            send(x_out, x_in.at[me], 3, (front, peer(offset)))
        base_out[...] = stream[0:ROWS]
        send(base_out, base_in, 10, (back, me))

        inverse = 1.0 / gain[...]
        arrived(x_in.at[pl.ds(0, GROUP - 1)], 3)
        y = jnp.concatenate([x_in[e] for e in range(GROUP)], axis=1)
        proj = dot(y, w_all[...])
        y = y.astype(f32)
        mixes = [jnp.sum(y * w_mix[c : c + 1], axis=1, keepdims=True) for c in range(4)]
        x = y * inverse
        squares = jnp.sum(x * x, axis=1, keepdims=True)
        scale = lax.rsqrt(squares * (1.0 / D) + norm_eps)
        proj = proj * scale
        mixes = [mix * scale for mix in mixes]

        def unit(x):
            return x * lax.rsqrt(jnp.sum(x * x, axis=1, keepdims=True) + norm_eps)

        dq = unit(proj[:, 0:128])
        dk = unit(proj[:, 128:256])
        value = jnp.concatenate([proj[:, 256:384], proj[:, 512:640]], axis=1)
        zgate = jnp.concatenate([proj[:, 384:512], proj[:, 640:768]], axis=1)
        wide = (BOTH, 2 * 128)
        high = iota(wide, 1) >= 128
        beta = jnp.where(high, jax.nn.sigmoid(mixes[1]), jax.nn.sigmoid(mixes[0]))

        def decay_of(h):
            t = mixes[2 + h] + dt_bias[h]
            soft = jnp.maximum(t, 0.0) + jnp.log(1.0 + jnp.exp(-jnp.abs(t)))
            return jnp.exp(-decay_scale[h] * soft)

        decay = jnp.where(high, decay_of(1), decay_of(0))

        arrived(s_in, 1)
        for g in range(2):
            for r in range(REQS):
                rows = s_in[:, g, r * 16 : (r + 1) * 16].astype(f32).reshape(GROUP, 2, 8, 128)
                blocks = [rows[j, h] for h in range(2) for j in range(GROUP)]
                held_states[g * REQS + r] = jnp.concatenate(blocks, axis=0).astype(bf16)

        both = jnp.concatenate([dk, dq], axis=0).astype(bf16)
        row_of = lax.rem(iota((2 * BOTH, 2 * 128), 0) // STEPS, 2 * REQS)
        prior = jnp.zeros((2 * BOTH, 2 * 128), f32)
        for r in range(2 * REQS):
            prior = jnp.where(row_of == r, dot_t(both, held_states[r]), prior)
        prior_k, prior_q = prior[:BOTH], prior[BOTH:]
        step = lax.rem(iota(wide, 0), STEPS)
        ratio = [jnp.ones(wide, f32), decay]
        for o in range(1, STEPS):
            ratio.append(decay * shifted(ratio[o], 1))
        whole = jnp.where(
            step == 0, ratio[1], jnp.where(step == 1, ratio[2], jnp.where(step == 2, ratio[3], ratio[4]))
        )
        key_back = [shifted(dk, o) for o in range(STEPS)]
        beta_prior = beta * (value - whole * prior_k)
        coupling = [
            jnp.where(step >= o, beta * ratio[o] * jnp.sum(dk * key_back[o], axis=1, keepdims=True), 0.0)
            for o in range(1, STEPS)
        ]
        update = beta_prior
        for _ in range(STEPS - 1):
            following = beta_prior
            for o in range(1, STEPS):
                following = following - coupling[o - 1] * shifted(update, o)
            update = following
        readout = whole * prior_q
        for o in range(STEPS):
            reach = jnp.sum(dq * key_back[o], axis=1, keepdims=True)
            readout = readout + jnp.where(step >= o, ratio[o] * reach, 0.0) * shifted(update, o)
        readout = readout * (128 ** -0.5)

        def normal(x):
            return x * lax.rsqrt(jnp.mean(x * x, axis=1, keepdims=True) + norm_eps) * dgain[...]

        normalized = jnp.concatenate([normal(readout[:, :128]), normal(readout[:, 128:])], axis=1)
        normalized = (normalized * zgate * jax.nn.sigmoid(zgate)).astype(bf16)

        total = dot(normalized, wdo[...])
        for e in range(GROUP):
            d_out[:, e] = total[:, e * SHARE : (e + 1) * SHARE].astype(bf16).reshape(2, ROWS, SHARE)
        for n, offset in enumerate(FAR_FIRST):
            other = peer(offset)
            send(d_out.at[1, other], d_in.at[n], 4, (front, other))
        for n, offset in enumerate(FAR_FIRST):
            other = peer(offset)
            send(d_out.at[0, other], d_in.at[n], 4, (back, other))
        send(d_out.at[0, me], d_in.at[GROUP - 1], 4, (back, me))
        result = stream[ROWS:BOTH] + d_out[1, me].astype(f32)
        sent(m_in.at[pl.ds(0, GROUP - 1), 0], 0)
        sent(s_more, 5)
        for r in range(1, LEVELS):

            @pl.when(my_rank == r)
            def _():
                sent(s_out.at[pl.ds(0, 2 * r)], 1)

        sent(a_in, 2)
        sent(x_in.at[pl.ds(0, GROUP - 1)], 3)
        sent(base_out, 10)
        arrived(d_in.at[pl.ds(0, GROUP - 1)], 4)
        for n in range(GROUP - 1):
            result = result + d_in[n].astype(f32)
        out_ref[...] = result
        sent(d_out.at[0], 4)
        sent(d_out.at[1, pl.ds(0, GROUP - 1)], 4)


def body(
    kv_pool, page_owner, page_slot, lengths, queries, gates, new_kv, tokens, attn_gain, out_heads,
    w_query_key, w_value_gate, w_beta_decay, decay_scale, dt_bias, delta_gain, w_delta_out, prior_state,
):
    hbm = pl.BlockSpec(memory_space=pl.ANY)
    smem = pl.BlockSpec(memory_space=pltpu.SMEM)
    vmem = pltpu.VMEM
    operands = (
        (kv_pool.reshape(SLOTS, 2, PAGE, KVH * HD), hbm),
        (page_owner, hbm),
        (page_slot, hbm),
        (lengths.reshape(REQS), smem),
        (queries.reshape(ROWS * GROUP, HD), hbm),
        (gates.reshape(ROWS, GROUP, HD), hbm),
        (new_kv.reshape(ROWS, 2, KVH, HD), hbm),
        (tokens, hbm),
        (attn_gain.reshape(1, D), hbm),
        (out_heads.reshape(HD, D), hbm),
        (w_query_key.reshape(2 * D, 128), hbm),
        (w_value_gate.reshape(4 * D, 128), hbm),
        (w_beta_decay.transpose(1, 2, 0), hbm),
        (decay_scale, smem),
        (dt_bias, smem),
        (delta_gain.reshape(1, 128), hbm),
        (w_delta_out.reshape(2 * 128, D), hbm),
        (prior_state, hbm),
    )
    out = pl.pallas_call(
        kernel,
        out_shape=jax.ShapeDtypeStruct((ROWS, SHARE), f32),
        in_specs=[spec for _, spec in operands],
        out_specs=pl.BlockSpec(memory_space=pltpu.VMEM),
        scratch_shapes=[
            vmem((KVH, 2, SLOTS, PAGE, HD), f32),
            vmem((REQS, 1, PAGES), jnp.int32),
            vmem((REQS, 1, PAGES), jnp.int32),
            vmem((2, ROWS * GROUP, 128), f32),
            vmem((ROWS, GROUP, HD), bf16),
            vmem((ROWS, 2, KVH, HD), f32),
            vmem((2, REQS, STEPS, SHARE), bf16),
            vmem((1, D), f32),
            vmem((HD, D), bf16),
            vmem((2 * D, 128), bf16),
            vmem((4 * D, 128), bf16),
            vmem((2, 2, D), bf16),
            vmem((1, 128), f32),
            vmem((2 * 128, D), bf16),
            vmem((REQS, GROUP, 2, 8, 128), f32),
            vmem((512, 128), f32),
            vmem((1024, 128), f32),
            vmem((D, 6 * 128), bf16),
            vmem((8, D), f32),
            vmem((GROUP, 64, 128), bf16),
            vmem((GROUP, 64, 128), bf16),
            vmem((GROUP, 2, 64, 128), bf16),
            vmem((2 * REQS, 256, 128), bf16),
            vmem((GROUP, ROWS, MSG), bf16),
            vmem((GROUP + 1, 2, ROWS, MSG), bf16),
            vmem((ROWS, MSG), bf16),
            vmem((ROWS, HD), bf16),
            vmem((ROWS, HD), bf16),
            vmem((GROUP, BOTH, SHARE), bf16),
            vmem((GROUP - 1, BOTH, SHARE), bf16),
            vmem((BOTH, SHARE), bf16),
            vmem((GROUP, BOTH, SHARE), bf16),
            vmem((2, GROUP, ROWS, SHARE), bf16),
            vmem((GROUP, ROWS, SHARE), bf16),
            vmem((ROWS, SHARE), f32),
            vmem((ROWS, SHARE), f32),
            pltpu.SemaphoreType.DMA((20,)),
            pltpu.SemaphoreType.DMA((11,)),
            pltpu.SemaphoreType.DMA((11,)),
            pltpu.SemaphoreType.REGULAR((LEVELS,)),
        ],
        compiler_params=pltpu.CompilerParams(
            collective_id=0, has_side_effects=True, vmem_limit_bytes=60 * 1024 * 1024
        ),
    )(*[value for value, _ in operands])
    return out.reshape(REQS, 1, STEPS, SHARE)


def solution(mesh):
    return jax.shard_map(
        body,
        mesh=mesh,
        in_specs=(
            P("req", "seq", None, None, None),
            P(None, "req", None),
            P(None, "req", None),
            P(None, "req"),
            P(None, "req", None, None, None),
            P(None, "req", None, None, None),
            P(None, "req", None, None, None, None),
            P(None, "req", None, None),
            P(),
            P("seq", None, None),
            P(None, "seq", None, None),
            P(None, "seq", None, None),
            P(None, None, "seq"),
            P("seq"),
            P("seq"),
            P(),
            P("seq", None, None),
            P(None, None, "req", "seq", None),
        ),
        out_specs=P(None, "req", None, "seq"),
        check_vma=False,
    )
```
